32 devices in a mesh: ctx: 16 (over z, x, core), head: 2 (over y).
Axes of the slice: x: 2, y: 2, z: 4, core: 2. Of those that a mesh axis runs over, the one named last changes fastest.
Arguments:
- query_raw: bfloat16 [2048, 2048], P('ctx', 'head'), may hold values from -6 to 6
- key_raw: bfloat16 [2048, 2048], P('ctx', 'head'), may hold values from -6 to 6
- value_raw: bfloat16 [2048, 4096], P('ctx', 'head'), may hold values from -6 to 6
- query_key_conv: bfloat16 [2, 4, 2048], P(None, None, 'head'), may hold values from -3 to 3
- value_conv: bfloat16 [4, 4096], P(None, 'head'), may hold values from -3 to 3
- output_gate: bfloat16 [2048, 4096], P('ctx', 'head'), may hold values from -6 to 6
- beta_logit: float32 [2048, 32], P('ctx', 'head')
- gate_logit: float32 [2048, 32], P('ctx', 'head')
- log_rate: float32 [32], P('head')
- norm_gain: float32 [128], replicated, may hold values from 0.5 to 2
- out_weight: bfloat16 [4096, 2048], P('head'), may hold values from -0.09375 to 0.09375
Outputs:
- mixed: bfloat16 [2048, 2048], P(('ctx', 'head'))
The draws below stay inside these ranges and needn't reach their ends.
All inputs are finite; a program needn't handle non-finite values.
Results may differ from the reference program's by a relative error of at most 0.022.
Values may be sent and summed in bfloat16 or wider, within the bound.
A program may use at most 128 MiB of HBM per device.

```python
import math
import jax
import jax.numpy as jnp
from jax import lax

D = 2048
VHEADS = 32
KHEADS = 16
HDIM = 128
CONV = 4
TOK_DEV = 128
TOKENS = 2048
N_HEAD = 2


def slow_heads(key):
    sub = jax.random.fold_in(key, 11)
    share = 0.5
    return jax.random.uniform(sub, (VHEADS,), jnp.float32) < share


def draw_log_rate(key, part):
    slow = slow_heads(key)
    jitter = jax.random.uniform(jax.random.fold_in(key, 12), (VHEADS,), jnp.float32, -0.3, 0.3)
    fast_level = math.log(TOKENS / 24.0)
    return jnp.where(slow, jitter, fast_level + jitter).astype(jnp.float32)


def draw_gate_logit(key, part):
    base_offset = math.log(0.25 / TOKENS) + jax.random.uniform(jax.random.fold_in(key, 21), (TOKENS, VHEADS), jnp.float32, -1.0, 1.0)
    position_list = jax.random.randint(jax.random.fold_in(key, 22), (3, VHEADS), 0, TOKENS)
    step_count = jnp.arange(TOKENS, dtype=jnp.int32)
    token_group = jnp.any(step_count[:, None, None] == position_list[None, :, :], axis=1)
    strong_decay = jax.random.uniform(jax.random.fold_in(key, 23), (TOKENS, VHEADS), jnp.float32, -1.5, -0.5)
    return jnp.where(token_group, strong_decay, base_offset).astype(jnp.float32)


def draw_beta_logit(key, part):
    slow = slow_heads(key)
    reach = jax.random.uniform(jax.random.fold_in(key, 33), (VHEADS,), jnp.float32, math.log(2.0), math.log(12.0))
    level = math.log(HDIM / TOK_DEV) - reach
    small = level[None, :] + jax.random.uniform(jax.random.fold_in(key, 31), (TOKENS, VHEADS), jnp.float32, -1.0, 1.0)
    broad = jax.random.uniform(jax.random.fold_in(key, 32), (TOKENS, VHEADS), jnp.float32, -2.0, 2.0)
    return jnp.where(slow[None, :], small, broad).astype(jnp.float32)


def block_levels(own_key, shape, split, low, high):
    factor_of = 1.0
    for axis_at, blocks in split:
        steps = jax.random.uniform(jax.random.fold_in(jax.random.fold_in(own_key, 6), axis_at), (blocks,), jnp.float32, low / len(split), high / len(split))
        factor_of = factor_of * jnp.repeat(jnp.exp(steps), shape[axis_at] // blocks).reshape((-1,) + (1,) * (len(shape) - 1 - axis_at))
    return factor_of


def normal_values(key, shape, deviation, most, cuts=(), held_as=jnp.bfloat16):
    level = block_levels(key, shape, cuts, -0.22, 0.18) if cuts else 1.0
    array = jax.random.normal(key, shape, jnp.float32) * deviation * level
    return jnp.minimum(jnp.maximum(array, -most), most).astype(held_as)


def setup_inputs(seed: int = 0) -> dict:
    arg_keys = jax.random.split(jax.random.key(seed), 12)
    return {
        "query_raw": normal_values(arg_keys[0], (TOKENS, KHEADS * HDIM), 1.0, 6.0, ((0, 16), (1, 2))),
        "key_raw": normal_values(arg_keys[1], (TOKENS, KHEADS * HDIM), 1.0, 6.0, ((0, 16), (1, 2))),
        "value_raw": normal_values(arg_keys[2], (TOKENS, VHEADS * HDIM), 1.0, 6.0, ((0, 16), (1, 2))),
        "query_key_conv": normal_values(arg_keys[3], (2, CONV, KHEADS * HDIM), CONV ** -0.5, 3.0, ((2, 2),)),
        "value_conv": normal_values(arg_keys[4], (CONV, VHEADS * HDIM), CONV ** -0.5, 3.0, ((1, 2),)),
        "output_gate": normal_values(arg_keys[5], (TOKENS, VHEADS * HDIM), 1.0, 6.0, ((0, 16), (1, 2))),
        "beta_logit": draw_beta_logit(jax.random.fold_in(arg_keys[11], 71), 0),
        "gate_logit": draw_gate_logit(jax.random.fold_in(arg_keys[11], 71), 0),
        "log_rate": draw_log_rate(jax.random.fold_in(arg_keys[11], 71), 0),
        "norm_gain": jnp.clip(jnp.exp(jax.random.uniform(arg_keys[9], (HDIM,), jnp.float32, math.log(0.5), math.log(2.0))), 0.5, 2.0),
        "out_weight": normal_values(arg_keys[10], (VHEADS * HDIM, D), (VHEADS * HDIM) ** -0.5, 0.09375, ((0, 2),)),
    }


def conv_silu(raw_rows, taps):
    values = raw_rows.astype(jnp.float32)
    padded = jnp.pad(values, ((CONV - 1, 0), (0, 0)))
    total = jnp.zeros_like(values)
    for offset in range(CONV):
        total = total + taps[offset].astype(jnp.float32) * padded[offset:offset + values.shape[0]]
    return jax.nn.silu(total)

def unit_rows(values):
    return values / jnp.sqrt(lax.optimization_barrier(jnp.sum(values * values, axis=-1, keepdims=True)) + 1e-06)

def reference(query_raw, key_raw, value_raw, query_key_conv, value_conv, output_gate, beta_logit, gate_logit, log_rate, norm_gain, out_weight):
    highest_precision = lax.Precision.HIGHEST
    ratio = VHEADS // KHEADS
    query = unit_rows(conv_silu(query_raw, query_key_conv[0]).reshape(TOKENS, KHEADS, HDIM)) * HDIM ** (-0.5)
    key = unit_rows(conv_silu(key_raw, query_key_conv[1]).reshape(TOKENS, KHEADS, HDIM))
    value = conv_silu(value_raw, value_conv).reshape(TOKENS, VHEADS, HDIM)
    query = jnp.repeat(query, ratio, axis=1)
    key = jnp.repeat(key, ratio, axis=1)
    beta = jax.nn.sigmoid(beta_logit)
    decay = -jnp.exp(log_rate)[None, :] * jax.nn.softplus(gate_logit)

    def advance(memory_state, inputs):
        query_transposed, key_transposed, value_t, beta_t, decay_t = inputs
        memory_state = memory_state * jnp.exp(decay_t)[:, None, None]
        retrieved_value = jnp.einsum('ne,nec->nc', key_transposed, memory_state, precision=highest_precision)
        memory_state = memory_state + beta_t[:, None, None] * key_transposed[:, :, None] * (value_t - retrieved_value)[:, None, :]
        core_matrix = jnp.einsum('ne,nec->nc', query_transposed, memory_state, precision=highest_precision)
        return (memory_state, core_matrix)
    start = jnp.zeros((VHEADS, HDIM, HDIM), jnp.float32)
    _, core = lax.scan(advance, start, (query, key, value, beta, decay))
    meansq = lax.optimization_barrier(jnp.mean(core * core, axis=-1, keepdims=True))
    gate = jax.nn.silu(output_gate.reshape(TOKENS, VHEADS, HDIM).astype(jnp.float32))
    normed = (core / jnp.sqrt(meansq + 1e-06) * norm_gain * gate).astype(jnp.bfloat16)
    normed = normed.reshape(TOKENS, VHEADS * HDIM)
    group = VHEADS * HDIM // N_HEAD
    total = jnp.zeros((TOKENS, D), jnp.float32)
    for index in range(N_HEAD):
        partial_value = jnp.dot(normed[:, index * group:(index + 1) * group], out_weight[index * group:(index + 1) * group], preferred_element_type=jnp.float32)
        partial_value = lax.optimization_barrier(partial_value.astype(jnp.bfloat16))
        total = total + partial_value.astype(jnp.float32)
    return total.astype(jnp.bfloat16)
```

```python
import functools

import jax
import jax.numpy as jnp
from jax import lax
from jax.experimental import pallas as pl
from jax.experimental.pallas import tpu as pltpu
from jax.sharding import PartitionSpec as P

HDIM = 128
CONV = 4
RIM = 16
MESH = pl.DeviceIdType.MESH
F32 = jnp.float32
BF16 = jnp.bfloat16


def mm(left, right):
    return jnp.dot(left.astype(BF16), right.astype(BF16), preferred_element_type=F32)


def mm_exact(left, right):
    return jnp.dot(left, right, precision=lax.Precision.HIGHEST, preferred_element_type=F32)


def silu(values):
    return values / (1.0 + jnp.exp(-values))


def unit_inverse(lower, row, col):
    pair = ((row ^ 1) == col) & (col < row)
    inverse = jnp.where(row == col, 1.0, 0.0) - jnp.where(pair, lower, 0.0)
    size = 2
    while size < lower.shape[0]:
        mask = (row // (2 * size) == col // (2 * size)) & (row // size > col // size)
        narrow = inverse.astype(BF16)
        step = mm(jnp.where(mask, lower, 0.0), narrow)
        inverse = inverse - mm(narrow, step)
        size *= 2
    return inverse


def layer_kernel(
    n_ctx,
    n_head,
    q_ref,
    k_ref,
    v_ref,
    qk_taps_ref,
    v_taps_ref,
    gate_ref,
    beta_ref,
    rate_ref,
    log_rate_ref,
    gain_ref,
    w_hbm,
    out_ref,
    ext,
    rim_q,
    rim_k,
    rim_v,
    taps,
    square,
    gamma_rows,
    beta_rows,
    map_ref,
    push_ref,
    lift_ref,
    local_ref,
    last_ref,
    state_in,
    state_out,
    total,
    part,
    part_in,
    w_ref,
    w_sem,
    rim_send,
    rim_recv,
    state_send,
    state_recv,
    part_send,
    part_recv,
):
    ctx = lax.axis_index("ctx")
    head = lax.axis_index("head")
    length = q_ref.shape[0]
    qk_width = q_ref.shape[1]
    v_width = v_ref.shape[1]
    heads = v_width // HDIM
    ratio = v_width // qk_width
    rows_out = length // n_head
    has_next = ctx < n_ctx - 1
    has_prev = ctx > 0
    after = jnp.minimum(ctx + 1, n_ctx - 1)
    before = jnp.maximum(ctx - 1, 0)

    w_copy = pltpu.make_async_copy(w_hbm, w_ref, w_sem)
    w_copy.start()

    barrier = pltpu.get_barrier_semaphore()

    @pl.when(has_next)
    def _():
        pl.semaphore_signal(barrier, inc=1, device_id=(after, head), device_id_type=MESH)

    @pl.when(has_prev)
    def _():
        pl.semaphore_signal(barrier, inc=1, device_id=(before, head), device_id_type=MESH)

    for hop in range(1, n_head):
        peer = lax.rem(head + hop, n_head)
        pl.semaphore_signal(barrier, inc=1, device_id=(ctx, peer), device_id_type=MESH)

    neighbours = has_next.astype(jnp.int32) + has_prev.astype(jnp.int32) + (n_head - 1)
    pl.semaphore_wait(barrier, neighbours)

    rims = [
        pltpu.make_async_remote_copy(
            src_ref=src.at[pl.ds(length - RIM, RIM), :],
            dst_ref=dst,
            send_sem=rim_send.at[i],
            recv_sem=rim_recv.at[i],
            device_id=(after, head),
            device_id_type=MESH,
        )
        for i, (src, dst) in enumerate(((q_ref, rim_q), (k_ref, rim_k), (v_ref, rim_v)))
    ]

    @pl.when(has_next)
    def _():
        for copy in rims:
            copy.start()

    row = lax.broadcasted_iota(jnp.int32, (HDIM, HDIM), 0)
    col = lax.broadcasted_iota(jnp.int32, (HDIM, HDIM), 1)
    rate = rate_ref[...]
    soft = jnp.maximum(rate, 0.0) + jnp.log1p(jnp.exp(-jnp.abs(rate)))
    square[...] = jnp.zeros_like(square)
    square[:, 0:heads] = -jnp.exp(log_rate_ref[...]) * soft
    upper = jnp.where(row <= col, 1.0, 0.0)
    gamma_rows[...] = mm_exact(square[...].T, upper)
    square[:, 0:heads] = 1.0 / (1.0 + jnp.exp(-beta_ref[...]))
    beta_rows[...] = square[...].T
    taps[:, 0:qk_width] = qk_taps_ref[0].astype(F32)
    taps[:, qk_width : 2 * qk_width] = qk_taps_ref[1].astype(F32)
    taps[:, 2 * qk_width :] = v_taps_ref[...].astype(F32)
    spans = ((q_ref, rim_q, 0), (k_ref, rim_k, qk_width), (v_ref, rim_v, 2 * qk_width))
    for ref, _, start in spans:
        ext[8 : 8 + length, start : start + ref.shape[1]] = ref[...].astype(F32)

    @pl.when(has_prev)
    def _():
        for copy in rims:
            copy.wait_recv()
        for _, rim, start in spans:
            ext[0:8, start : start + rim.shape[1]] = rim[...].astype(F32)[RIM - 8 : RIM]

    @pl.when(jnp.logical_not(has_prev))
    def _():
        ext[0:8, :] = jnp.zeros((8, ext.shape[1]), F32)

    def conv(start):
        at = pl.ds(pl.multiple_of(start, HDIM), HDIM)
        result = taps[0:1, at] * ext[5 : 5 + length, at]
        for offset in range(1, CONV):
            result += taps[offset : offset + 1, at] * ext[5 + offset : 5 + offset + length, at]
        return silu(result)

    def unit(values):
        return values * lax.rsqrt(jnp.sum(values * values, axis=-1, keepdims=True) + 1e-06)

    key_group = 2 if (heads // ratio) % 2 == 0 else 1

    def local_step(group, _):
        for own in range(key_group):
            key_head = group * key_group + own
            query = unit(conv(key_head * HDIM)) * HDIM ** (-0.5)
            key = unit(conv(qk_width + key_head * HDIM))
            key_t = key.T
            key_key = mm(key, key_t)
            query_key = mm(query, key_t)
            for sub in range(ratio):
                h = key_head * ratio + sub
                value = conv(2 * qk_width + h * HDIM)
                gamma_r = gamma_rows[pl.ds(h, 1), :]
                beta_r = beta_rows[pl.ds(h, 1), :]
                gamma_c = jnp.broadcast_to(gamma_r, (HDIM, HDIM)).T
                upto = row >= col
                ratio_decay = jnp.exp(jnp.where(upto, gamma_c - gamma_r, 0.0)) * beta_r
                lower = jnp.where(row > col, ratio_decay * key_key, 0.0)
                scores = jnp.where(upto, ratio_decay * query_key, 0.0)
                growth = jnp.exp(gamma_c)
                inverse = unit_inverse(lower, row, col)
                solved = mm(inverse, jnp.concatenate([value, growth * key], axis=1))
                solved = solved.astype(BF16)
                raised = mm(scores, solved)
                last = gamma_c[HDIM - 1 : HDIM, :]
                tail = key_t * (jnp.exp(last - gamma_r) * beta_r)
                pushed = mm(tail, solved)
                map_ref[h] = pushed[:, HDIM:].astype(BF16)
                push_ref[h] = pushed[:, :HDIM]
                lift_ref[h] = (growth * query - raised[:, HDIM:]).astype(BF16)
                local_ref[h] = raised[:, :HDIM]
                last_ref[pl.ds(h, 1), :] = jnp.exp(last)
        return 0

    lax.fori_loop(0, heads // ratio // key_group, local_step, 0)

    @pl.when(jnp.logical_not(has_prev))
    def _():
        state_in[...] = jnp.zeros_like(state_in)

    total[...] = jnp.zeros_like(total)
    w_copy.wait()

    def state_copy(h):
        return pltpu.make_async_remote_copy(
            src_ref=state_out.at[h],
            dst_ref=state_in.at[h],
            send_sem=state_send.at[h],
            recv_sem=state_recv.at[h],
            device_id=(after, head),
            device_id_type=MESH,
        )

    def normed_head(h):
        @pl.when(has_prev)
        def _():
            state_copy(h).wait_recv()

        before_state = state_in[h]

        @pl.when(has_next)
        def _():
            moved = jnp.dot(map_ref[h], before_state, preferred_element_type=F32)
            grown = last_ref[pl.ds(h, 1), :] * before_state.astype(F32)
            state_out[h] = (grown - moved + push_ref[h]).astype(BF16)
            state_copy(h).start()

        core = local_ref[h] + jnp.dot(lift_ref[h], before_state, preferred_element_type=F32)
        scale = lax.rsqrt(jnp.mean(core * core, axis=-1, keepdims=True) + 1e-06)
        at = pl.ds(pl.multiple_of(h * HDIM, HDIM), HDIM)
        gate = silu(gate_ref[:, at].astype(F32))
        return (core * scale * gain_ref[...] * gate).astype(BF16)

    pairs = heads // 2

    def pair_rows(pair):
        return pl.ds(pl.multiple_of(pair * (2 * HDIM), 2 * HDIM), 2 * HDIM)

    def sweep(pair, _):
        normed = jnp.concatenate([normed_head(2 * pair), normed_head(2 * pair + 1)], axis=1)
        total[...] += jnp.dot(normed, w_ref[pair_rows(pair), :], preferred_element_type=F32)
        return 0

    lax.fori_loop(0, pairs, sweep, 0)
    part[...] = total[...].astype(BF16)

    copies = []
    for hop in range(1, n_head):
        peer = lax.rem(head + hop, n_head)
        copy = pltpu.make_async_remote_copy(
            src_ref=part.at[pl.ds(pl.multiple_of(peer * rows_out, 16), rows_out), :],
            dst_ref=part_in.at[hop - 1],
            send_sem=part_send.at[hop - 1],
            recv_sem=part_recv.at[hop - 1],
            device_id=(ctx, peer),
            device_id_type=MESH,
        )
        copy.start()
        copies.append(copy)
    mixed = part[pl.ds(pl.multiple_of(head * rows_out, 16), rows_out), :].astype(F32)
    for hop, copy in enumerate(copies):
        copy.wait_recv()
        mixed += part_in[hop].astype(F32)
    out_ref[...] = mixed.astype(BF16)

    for copy in copies:
        copy.wait_send()

    @pl.when(has_next)
    def _():
        for copy in rims:
            copy.wait_send()

        def drain(h, _):
            state_copy(h).wait_send()
            return 0

        lax.fori_loop(0, heads, drain, 0)


def local(n_ctx, n_head, *args):
    (q, k, v, qk_taps, v_taps, gate, beta, rate, log_rate, gain, weight) = args
    length, qk_width = q.shape
    v_width = v.shape[1]
    heads = v_width // HDIM
    model = weight.shape[1]
    rows_out = length // n_head
    width = 2 * qk_width + v_width
    vmem = pl.BlockSpec(memory_space=pltpu.VMEM)
    dma = pltpu.SemaphoreType.DMA
    blocks = (heads, HDIM, HDIM)
    peers = max(n_head - 1, 1)
    return pl.pallas_call(
        functools.partial(layer_kernel, n_ctx, n_head),
        out_shape=jax.ShapeDtypeStruct((rows_out, model), BF16),
        in_specs=[vmem] * 10 + [pl.BlockSpec(memory_space=pl.ANY)],
        out_specs=vmem,
        scratch_shapes=[
            pltpu.VMEM((8 + length, width), F32),
            pltpu.VMEM((RIM, qk_width), BF16),
            pltpu.VMEM((RIM, qk_width), BF16),
            pltpu.VMEM((RIM, v_width), BF16),
            pltpu.VMEM((CONV, width), F32),
            pltpu.VMEM((HDIM, HDIM), F32),
            pltpu.VMEM((HDIM, HDIM), F32),
            pltpu.VMEM((HDIM, HDIM), F32),
            pltpu.VMEM(blocks, BF16),
            pltpu.VMEM(blocks, F32),
            pltpu.VMEM(blocks, BF16),
            pltpu.VMEM(blocks, F32),
            pltpu.VMEM((heads, HDIM), F32),
            pltpu.VMEM(blocks, BF16),
            pltpu.VMEM(blocks, BF16),
            pltpu.VMEM((length, model), F32),
            pltpu.VMEM((length, model), BF16),
            pltpu.VMEM((peers, rows_out, model), BF16),
            pltpu.VMEM(weight.shape, BF16),
            dma,
            dma((3,)),
            dma((3,)),
            dma((heads,)),
            dma((heads,)),
            dma((peers,)),
            dma((peers,)),
        ],
        compiler_params=pltpu.CompilerParams(
            collective_id=0, has_side_effects=True, vmem_limit_bytes=48 * 2**20
        ),
    )(q, k, v, qk_taps, v_taps, gate, beta, rate, log_rate[None, :], gain[None, :], weight)


def solution(mesh):
    in_specs = (
        P("ctx", "head"),
        P("ctx", "head"),
        P("ctx", "head"),
        P(None, None, "head"),
        P(None, "head"),
        P("ctx", "head"),
        P("ctx", "head"),
        P("ctx", "head"),
        P("head"),
        P(),
        P("head", None),
    )
    out_specs = P(("ctx", "head"), None)
    return jax.shard_map(
        functools.partial(local, mesh.shape["ctx"], mesh.shape["head"]),
        mesh=mesh,
        in_specs=in_specs,
        out_specs=out_specs,
        check_vma=False,
    )
```

```python
import functools

import jax
import jax.numpy as jnp
from jax import lax
from jax.experimental import pallas as pl
from jax.experimental.pallas import tpu as pltpu
from jax.sharding import PartitionSpec as P

HDIM = 128
CONV = 4
RIM = 16
MESH = pl.DeviceIdType.MESH
F32 = jnp.float32
BF16 = jnp.bfloat16


def mm(left, right):
    return jnp.dot(left.astype(BF16), right.astype(BF16), preferred_element_type=F32)


def mm_exact(left, right):
    return jnp.dot(left, right, precision=lax.Precision.HIGHEST, preferred_element_type=F32)


def silu(values):
    return values / (1.0 + jnp.exp(-values))


def unit_inverses(lowers, masks, eye):
    span = lowers[0].shape[0]
    inverses = [eye - lower * masks[0] for lower in lowers]
    level, size = 1, 2
    while size < span:
        mask = masks[level]
        if size < RIM:
            steps = [mm(low * mask, inv).astype(BF16) for low, inv in zip(lowers, inverses)]
            news = [mm(inv, step).astype(BF16) for inv, step in zip(inverses, steps)]
            inverses = [inv - new for inv, new in zip(inverses, news)]
        else:
            cuts = [slice(at, at + size) for at in range(0, span, size)]

            def odd(values):
                return jnp.concatenate([values[cut] for cut in cuts[1::2]], axis=0)

            odd_mask = odd(mask)
            halves = [mm(odd(low) * odd_mask, inv).astype(BF16) for low, inv in zip(lowers, inverses)]
            gap = jnp.zeros((size, span), BF16)
            steps = [
                jnp.concatenate(
                    [part for at in range(0, span // 2, size) for part in (gap, half[at : at + size])],
                    axis=0,
                )
                for half in halves
            ]
            odds = [odd(inv) for inv in inverses]
            news = [own - mm(own, step).astype(BF16) for own, step in zip(odds, steps)]
            inverses = [
                jnp.concatenate(
                    [
                        part
                        for i, cut in enumerate(cuts[0::2])
                        for part in (inv[cut], new[i * size : (i + 1) * size])
                    ],
                    axis=0,
                )
                for inv, new in zip(inverses, news)
            ]
        level, size = level + 1, 2 * size
    return inverses


def largest(count, most):
    while count % most:
        most -= 1
    return most


def layer_kernel(
    n_ctx,
    n_head,
    q_hbm,
    k_hbm,
    v_hbm,
    qk_taps_hbm,
    v_taps_hbm,
    gate_hbm,
    beta_hbm,
    rate_hbm,
    log_rate_hbm,
    gain_hbm,
    w_hbm,
    out_ref,
    q_ref,
    k_ref,
    v_ref,
    qk_taps_ref,
    v_taps_ref,
    gate_ref,
    beta_ref,
    rate_ref,
    log_rate_ref,
    gain_ref,
    w_ref,
    in_sem,
    ext,
    rim_q,
    rim_k,
    rim_v,
    taps,
    square,
    masks_ref,
    gamma_rows,
    beta_rows,
    map_ref,
    push_ref,
    lift_ref,
    local_ref,
    last_ref,
    state_in,
    state_out,
    gates,
    total,
    part,
    part_in,
    rim_send,
    rim_recv,
    state_send,
    state_recv,
    part_send,
    part_recv,
):
    ctx = lax.axis_index("ctx")
    head = lax.axis_index("head")
    length = q_ref.shape[0]
    qk_width = q_ref.shape[1]
    v_width = v_ref.shape[1]
    heads = v_width // HDIM
    ratio = v_width // qk_width
    rows_out = length // n_head
    chunks, _, chunk_width = part.shape
    has_next = ctx < n_ctx - 1
    has_prev = ctx > 0
    early = ctx < n_ctx // 2
    after = jnp.minimum(ctx + 1, n_ctx - 1)
    before = jnp.maximum(ctx - 1, 0)

    barrier = pltpu.get_barrier_semaphore()

    @pl.when(has_next)
    def _():
        pl.semaphore_signal(barrier, inc=1, device_id=(after, head), device_id_type=MESH)

    @pl.when(has_prev)
    def _():
        pl.semaphore_signal(barrier, inc=1, device_id=(before, head), device_id_type=MESH)

    for hop in range(1, n_head):
        peer = lax.rem(head + hop, n_head)
        pl.semaphore_signal(barrier, inc=1, device_id=(ctx, peer), device_id_type=MESH)

    ins = [
        pltpu.make_async_copy(src, dst, in_sem.at[i])
        for i, (src, dst) in enumerate(
            (
                (rate_hbm, rate_ref),
                (log_rate_hbm, log_rate_ref),
                (beta_hbm, beta_ref),
                (qk_taps_hbm, qk_taps_ref),
                (v_taps_hbm, v_taps_ref),
                (q_hbm, q_ref),
                (k_hbm, k_ref),
                (v_hbm, v_ref),
                (gain_hbm, gain_ref),
                (gate_hbm, gate_ref),
                (w_hbm, w_ref),
            )
        )
    ]
    for copy in ins:
        copy.start()

    neighbours = has_next.astype(jnp.int32) + has_prev.astype(jnp.int32) + (n_head - 1)
    pl.semaphore_wait(barrier, neighbours)

    rims = [
        pltpu.make_async_remote_copy(
            src_ref=src.at[pl.ds(length - RIM, RIM), :],
            dst_ref=dst,
            send_sem=rim_send.at[i],
            recv_sem=rim_recv.at[i],
            device_id=(after, head),
            device_id_type=MESH,
        )
        for i, (src, dst) in enumerate(((q_hbm, rim_q), (k_hbm, rim_k), (v_hbm, rim_v)))
    ]

    @pl.when(has_next)
    def _():
        for copy in rims:
            copy.start()

    row = lax.broadcasted_iota(jnp.int32, (HDIM, HDIM), 0)
    col = lax.broadcasted_iota(jnp.int32, (HDIM, HDIM), 1)
    size = 1
    for level in range(masks_ref.shape[0]):
        inside = (row // (2 * size) == col // (2 * size)) & (row // size > col // size)
        masks_ref[level] = jnp.where(inside, 1.0, 0.0).astype(BF16)
        size *= 2
    for copy in ins[0:3]:
        copy.wait()
    rate = rate_ref[...]
    soft = jnp.maximum(rate, 0.0) + jnp.log1p(jnp.exp(-jnp.abs(rate)))
    square[...] = jnp.zeros_like(square)
    square[:, 0:heads] = jnp.broadcast_to(log_rate_ref[...], (HDIM, heads))
    decay = -jnp.exp(square[...].T[0:heads]) * soft
    upper = jnp.where(row <= col, 1.0, 0.0)
    gamma_rows[...] = mm_exact(decay, upper)
    beta_rows[...] = 1.0 / (1.0 + jnp.exp(-beta_ref[...]))
    for copy in ins[3:8]:
        copy.wait()
    taps[:, 0:qk_width] = qk_taps_ref[0].astype(F32)
    taps[:, qk_width : 2 * qk_width] = qk_taps_ref[1].astype(F32)
    taps[:, 2 * qk_width :] = v_taps_ref[...].astype(F32)
    spans = ((q_ref, rim_q, 0), (k_ref, rim_k, qk_width), (v_ref, rim_v, 2 * qk_width))
    for ref, _, start in spans:
        ext[8 : 8 + length, start : start + ref.shape[1]] = ref[...].astype(F32)

    @pl.when(has_prev)
    def _():
        for copy in rims:
            copy.wait_recv()
        for _, rim, start in spans:
            ext[0:8, start : start + rim.shape[1]] = rim[...].astype(F32)[RIM - 8 : RIM]

    @pl.when(jnp.logical_not(has_prev))
    def _():
        ext[0:8, :] = jnp.zeros((8, ext.shape[1]), F32)
        state_in[...] = jnp.zeros_like(state_in)

    def conv(start):
        at = pl.ds(pl.multiple_of(start, HDIM), HDIM)
        result = taps[0:1, at] * ext[5 : 5 + length, at]
        for offset in range(1, CONV):
            result += taps[offset : offset + 1, at] * ext[5 + offset : 5 + offset + length, at]
        return silu(result)

    def unit(values):
        return values * lax.rsqrt(jnp.sum(values * values, axis=-1, keepdims=True) + 1e-06)

    key_heads = heads // ratio
    key_group = largest(key_heads, 4)

    def local_step(group, _):
        owns = [group * key_group + i for i in range(key_group)]
        queries = [unit(conv(own * HDIM)) * HDIM ** (-0.5) for own in owns]
        keys = [unit(conv(qk_width + own * HDIM)) for own in owns]
        keys_t = [key.T for key in keys]
        key_keys = [mm(key, key_t) for key, key_t in zip(keys, keys_t)]
        query_keys = [mm(query, key_t) for query, key_t in zip(queries, keys_t)]
        upto = row >= col
        lowers, scores, rights, lifts, tails = [], [], [], [], []
        for i in range(key_group * ratio):
            h, k = group * (key_group * ratio) + i, i // ratio
            gamma_r = gamma_rows[pl.ds(h, 1), :]
            beta_r = beta_rows[pl.ds(h, 1), :]
            gamma_c = jnp.broadcast_to(gamma_r, (HDIM, HDIM)).T
            faded = jnp.exp(jnp.where(upto, gamma_c - gamma_r, 0.0)) * beta_r
            lowers.append(jnp.where(row > col, faded * key_keys[k], 0.0).astype(BF16))
            scores.append(jnp.where(upto, faded * query_keys[k], 0.0).astype(BF16))
            growth = jnp.exp(gamma_c)
            last = gamma_c[HDIM - 1 : HDIM, :]
            value = conv(2 * qk_width + h * HDIM)
            rights.append(jnp.concatenate([value, growth * keys[k]], axis=1).astype(BF16))
            lifts.append(growth * queries[k])
            tails.append((keys_t[k] * (jnp.exp(last - gamma_r) * beta_r)).astype(BF16))
            last_ref[pl.ds(h, 1), :] = jnp.exp(last)
        eye = jnp.where(row == col, 1.0, 0.0).astype(BF16)
        masks = [masks_ref[level] for level in range(masks_ref.shape[0])]
        inverses = unit_inverses(lowers, masks, eye)
        solved = [mm(inv, right).astype(BF16) for inv, right in zip(inverses, rights)]
        pushes = [mm(tail, one) for tail, one in zip(tails, solved)]
        raises = [mm(score, one) for score, one in zip(scores, solved)]
        for i in range(key_group * ratio):
            h = group * (key_group * ratio) + i
            map_ref[h] = pushes[i][:, HDIM:].astype(BF16)
            push_ref[h] = pushes[i][:, :HDIM]
            lift_ref[h] = (lifts[i] - raises[i][:, HDIM:]).astype(BF16)
            local_ref[h] = raises[i][:, :HDIM]
        return 0

    lax.fori_loop(0, key_heads // key_group, local_step, 0)

    def state_copy(h):
        return pltpu.make_async_remote_copy(
            src_ref=state_out.at[h],
            dst_ref=state_in.at[h],
            send_sem=state_send.at[h],
            recv_sem=state_recv.at[h],
            device_id=(after, head),
            device_id_type=MESH,
        )

    def forward(h):
        @pl.when(has_prev)
        def _():
            state_copy(h).wait_recv()

        @pl.when(has_next)
        def _():
            arrived = state_in[h]
            moved = jnp.dot(map_ref[h], arrived, preferred_element_type=F32)
            grown = last_ref[pl.ds(h, 1), :] * arrived.astype(F32)
            state_out[h] = (grown - moved + push_ref[h]).astype(BF16)
            state_copy(h).start()

    @pl.when(early)
    def _():
        def all_forward(h, _):
            forward(h)
            return 0

        lax.fori_loop(0, heads, all_forward, 0)

    for copy in ins[8:11]:
        copy.wait()

    def open_gate(h, _):
        at = pl.ds(pl.multiple_of(h * HDIM, HDIM), HDIM)
        gates[:, at] = gain_ref[...] * silu(gate_ref[:, at].astype(F32))
        return 0

    lax.fori_loop(0, heads, open_gate, 0)

    sweep_group = largest(heads, 4)
    sweeps = heads // sweep_group
    depth = sweep_group * HDIM

    def normed_group(group):
        first = group * sweep_group

        @pl.when(jnp.logical_not(early))
        def _():
            for i in range(sweep_group):
                forward(first + i)

        cores = [
            local_ref[first + i]
            + jnp.dot(lift_ref[first + i], state_in[first + i], preferred_element_type=F32)
            for i in range(sweep_group)
        ]
        scales = [lax.rsqrt(jnp.mean(core * core, axis=-1, keepdims=True) + 1e-06) for core in cores]
        normed = [
            core * scale * gates[:, pl.ds(pl.multiple_of((first + i) * HDIM, HDIM), HDIM)]
            for i, (core, scale) in enumerate(zip(cores, scales))
        ]
        return jnp.concatenate(normed, axis=1).astype(BF16)

    def product(normed, group, chunk):
        rows = pl.ds(pl.multiple_of(group * depth, depth), depth)
        weight = w_ref[rows, chunk * chunk_width : (chunk + 1) * chunk_width]
        return jnp.dot(normed, weight, preferred_element_type=F32)

    total[...] = jnp.zeros_like(total)

    def sweep(group, _):
        normed = normed_group(group)
        for chunk in range(chunks):
            total[chunk] += product(normed, group, chunk)
        return 0

    lax.fori_loop(0, sweeps - 1, sweep, 0)

    normed = normed_group(sweeps - 1)
    copies = []
    for chunk in range(chunks):
        part[chunk] = (total[chunk] + product(normed, sweeps - 1, chunk)).astype(BF16)
        for hop in range(1, n_head):
            peer = lax.rem(head + hop, n_head)
            copy = pltpu.make_async_remote_copy(
                src_ref=part.at[chunk, pl.ds(pl.multiple_of(peer * rows_out, 16), rows_out), :],
                dst_ref=part_in.at[hop - 1, chunk],
                send_sem=part_send.at[hop - 1, chunk],
                recv_sem=part_recv.at[hop - 1, chunk],
                device_id=(ctx, peer),
                device_id_type=MESH,
            )
            copy.start()
            copies.append((chunk, hop - 1, copy))
    kept = pl.ds(pl.multiple_of(head * rows_out, 16), rows_out)
    for chunk in range(chunks):
        mixed = part[chunk, kept, :].astype(F32)
        for own, hop, copy in copies:
            if own == chunk:
                copy.wait_recv()
                mixed += part_in[hop, chunk].astype(F32)
        out_ref[:, chunk * chunk_width : (chunk + 1) * chunk_width] = mixed.astype(BF16)

    for _, _, copy in copies:
        copy.wait_send()

    @pl.when(has_next)
    def _():
        for copy in rims:
            copy.wait_send()

        def drain(h, _):
            state_copy(h).wait_send()
            return 0

        lax.fori_loop(0, heads, drain, 0)


def local(n_ctx, n_head, *args):
    (q, k, v, qk_taps, v_taps, gate, beta, rate, log_rate, gain, weight) = args
    length, qk_width = q.shape
    v_width = v.shape[1]
    heads = v_width // HDIM
    model = weight.shape[1]
    rows_out = length // n_head
    width = 2 * qk_width + v_width
    dma = pltpu.SemaphoreType.DMA
    blocks = (heads, HDIM, HDIM)
    peers = max(n_head - 1, 1)
    chunks = 4
    operands = (
        q, k, v, qk_taps, v_taps, gate, beta.T, rate.T, log_rate[None, :], gain[None, :], weight
    )
    return pl.pallas_call(
        functools.partial(layer_kernel, n_ctx, n_head),
        out_shape=jax.ShapeDtypeStruct((rows_out, model), BF16),
        in_specs=[pl.BlockSpec(memory_space=pl.ANY)] * len(operands),
        out_specs=pl.BlockSpec(memory_space=pltpu.VMEM),
        scratch_shapes=[
            *[pltpu.VMEM(operand.shape, operand.dtype) for operand in operands],
            dma((len(operands),)),
            pltpu.VMEM((8 + length, width), F32),
            pltpu.VMEM((RIM, qk_width), BF16),
            pltpu.VMEM((RIM, qk_width), BF16),
            pltpu.VMEM((RIM, v_width), BF16),
            pltpu.VMEM((CONV, width), F32),
            pltpu.VMEM((HDIM, HDIM), F32),
            pltpu.VMEM((HDIM.bit_length() - 1, HDIM, HDIM), BF16),
            pltpu.VMEM((heads, HDIM), F32),
            pltpu.VMEM((heads, HDIM), F32),
            pltpu.VMEM(blocks, BF16),
            pltpu.VMEM(blocks, F32),
            pltpu.VMEM(blocks, BF16),
            pltpu.VMEM(blocks, F32),
            pltpu.VMEM((heads, HDIM), F32),
            pltpu.VMEM(blocks, BF16),
            pltpu.VMEM(blocks, BF16),
            pltpu.VMEM((length, v_width), F32),
            pltpu.VMEM((chunks, length, model // chunks), F32),
            pltpu.VMEM((chunks, length, model // chunks), BF16),
            pltpu.VMEM((peers, chunks, rows_out, model // chunks), BF16),
            dma((3,)),
            dma((3,)),
            dma((heads,)),
            dma((heads,)),
            dma((peers, chunks)),
            dma((peers, chunks)),
        ],
        compiler_params=pltpu.CompilerParams(
            collective_id=0, has_side_effects=True, vmem_limit_bytes=60 * 2**20
        ),
    )(*operands)


def solution(mesh):
    in_specs = (
        P("ctx", "head"),
        P("ctx", "head"),
        P("ctx", "head"),
        P(None, None, "head"),
        P(None, "head"),
        P("ctx", "head"),
        P("ctx", "head"),
        P("ctx", "head"),
        P("head"),
        P(),
        P("head", None),
    )
    out_specs = P(("ctx", "head"), None)
    return jax.shard_map(
        functools.partial(local, mesh.shape["ctx"], mesh.shape["head"]),
        mesh=mesh,
        in_specs=in_specs,
        out_specs=out_specs,
        check_vma=False,
    )
```

```python
import functools

import jax
import jax.numpy as jnp
from jax import lax
from jax.experimental import pallas as pl
from jax.experimental.pallas import tpu as pltpu
from jax.sharding import PartitionSpec as P

HDIM = 128
CONV = 4
RIM = 16
PLANE = 4
MESH = pl.DeviceIdType.MESH
F32 = jnp.float32
BF16 = jnp.bfloat16


def mm(left, right):
    return jnp.dot(left.astype(BF16), right.astype(BF16), preferred_element_type=F32)


def mm_exact(left, right):
    return jnp.dot(left, right, precision=lax.Precision.HIGHEST, preferred_element_type=F32)


def silu(values):
    return values / (1.0 + jnp.exp(-values))


def unit_inverses(lowers, masks, eye):
    span = lowers[0].shape[0]
    inverses = [eye - lower * masks[0] for lower in lowers]
    level, size = 1, 2
    while size < span:
        mask = masks[level]
        if size < RIM:
            steps = [mm(low * mask, inv).astype(BF16) for low, inv in zip(lowers, inverses)]
            news = [mm(inv, step).astype(BF16) for inv, step in zip(inverses, steps)]
            inverses = [inv - new for inv, new in zip(inverses, news)]
        else:
            cuts = [slice(at, at + size) for at in range(0, span, size)]

            def odd(values):
                return jnp.concatenate([values[cut] for cut in cuts[1::2]], axis=0)

            odd_mask = odd(mask)
            halves = [mm(odd(low) * odd_mask, inv).astype(BF16) for low, inv in zip(lowers, inverses)]
            gap = jnp.zeros((size, span), BF16)
            steps = [
                jnp.concatenate(
                    [part for at in range(0, span // 2, size) for part in (gap, half[at : at + size])],
                    axis=0,
                )
                for half in halves
            ]
            odds = [odd(inv) for inv in inverses]
            news = [own - mm(own, step).astype(BF16) for own, step in zip(odds, steps)]
            inverses = [
                jnp.concatenate(
                    [
                        part
                        for i, cut in enumerate(cuts[0::2])
                        for part in (inv[cut], new[i * size : (i + 1) * size])
                    ],
                    axis=0,
                )
                for inv, new in zip(inverses, news)
            ]
        level, size = level + 1, 2 * size
    return inverses


def largest(count, most):
    while count % most:
        most -= 1
    return most


def layer_kernel(
    n_ctx,
    n_head,
    q_hbm,
    k_hbm,
    v_hbm,
    qk_taps_hbm,
    v_taps_hbm,
    gate_hbm,
    beta_hbm,
    rate_hbm,
    log_rate_hbm,
    gain_hbm,
    w_hbm,
    out_ref,
    q_ref,
    k_ref,
    v_ref,
    qk_taps_ref,
    v_taps_ref,
    gate_ref,
    beta_ref,
    rate_ref,
    log_rate_ref,
    gain_ref,
    w_ref,
    in_sem,
    ext,
    rim_q,
    rim_k,
    rim_v,
    taps,
    square,
    masks_ref,
    gamma_rows,
    beta_rows,
    map_ref,
    near_map,
    joined_out,
    joined_in,
    lift_ref,
    local_ref,
    entry,
    entry_out,
    state_in,
    mate_out,
    gates,
    total,
    part,
    part_in,
    rim_send,
    rim_recv,
    near_send,
    near_recv,
    joined_send,
    joined_recv,
    entry_send,
    entry_recv,
    fan_send,
    fan_recv,
    mate_send,
    mate_recv,
    part_send,
    part_recv,
):
    ctx = lax.axis_index("ctx")
    head = lax.axis_index("head")
    length = q_ref.shape[0]
    qk_width = q_ref.shape[1]
    v_width = v_ref.shape[1]
    heads = v_width // HDIM
    ratio = v_width // qk_width
    rows_out = length // n_head
    chunks, _, chunk_width = part.shape
    has_next = ctx < n_ctx - 1
    has_prev = ctx > 0
    place = lax.rem(ctx, PLANE)
    is_even = lax.rem(place, 2) == 0
    is_joiner = place == 1
    is_chain = place == PLANE - 1
    chain_next = is_chain & (ctx + PLANE < n_ctx)
    chain_prev = is_chain & (ctx >= PLANE)

    def at(offset):
        return (jnp.clip(ctx + offset, 0, n_ctx - 1), head)

    links = (
        (1, has_next),
        (-1, has_prev),
        (2, is_joiner),
        (-2, is_chain),
        (PLANE, chain_next),
        (-PLANE, chain_prev),
    )

    barrier = pltpu.get_barrier_semaphore()

    neighbours = n_head - 1
    for offset, there in links:
        neighbours += there.astype(jnp.int32)

        @pl.when(there)
        def _(offset=offset):
            pl.semaphore_signal(barrier, inc=1, device_id=at(offset), device_id_type=MESH)

    for hop in range(1, n_head):
        peer = lax.rem(head + hop, n_head)
        pl.semaphore_signal(barrier, inc=1, device_id=(ctx, peer), device_id_type=MESH)

    ins = [
        pltpu.make_async_copy(src, dst, in_sem.at[i])
        for i, (src, dst) in enumerate(
            (
                (rate_hbm, rate_ref),
                (log_rate_hbm, log_rate_ref),
                (beta_hbm, beta_ref),
                (qk_taps_hbm, qk_taps_ref),
                (v_taps_hbm, v_taps_ref),
                (q_hbm, q_ref),
                (k_hbm, k_ref),
                (v_hbm, v_ref),
                (gain_hbm, gain_ref),
                (gate_hbm, gate_ref),
                (w_hbm, w_ref),
            )
        )
    ]
    for copy in ins:
        copy.start()

    pl.semaphore_wait(barrier, neighbours)

    rims = [
        pltpu.make_async_remote_copy(
            src_ref=src.at[pl.ds(length - RIM, RIM), :],
            dst_ref=dst,
            send_sem=rim_send.at[i],
            recv_sem=rim_recv.at[i],
            device_id=at(1),
            device_id_type=MESH,
        )
        for i, (src, dst) in enumerate(((q_hbm, rim_q), (k_hbm, rim_k), (v_hbm, rim_v)))
    ]

    @pl.when(has_next)
    def _():
        for copy in rims:
            copy.start()

    row = lax.broadcasted_iota(jnp.int32, (HDIM, HDIM), 0)
    col = lax.broadcasted_iota(jnp.int32, (HDIM, HDIM), 1)
    size = 1
    for level in range(masks_ref.shape[0]):
        inside = (row // (2 * size) == col // (2 * size)) & (row // size > col // size)
        masks_ref[level] = jnp.where(inside, 1.0, 0.0).astype(BF16)
        size *= 2
    for copy in ins[0:3]:
        copy.wait()
    rate = rate_ref[...]
    soft = jnp.maximum(rate, 0.0) + jnp.log1p(jnp.exp(-jnp.abs(rate)))
    square[...] = jnp.zeros_like(square)
    square[:, 0:heads] = jnp.broadcast_to(log_rate_ref[...], (HDIM, heads))
    decay = -jnp.exp(square[...].T[0:heads]) * soft
    upper = jnp.where(row <= col, 1.0, 0.0)
    gamma_rows[...] = mm_exact(decay, upper)
    beta_rows[...] = 1.0 / (1.0 + jnp.exp(-beta_ref[...]))
    for copy in ins[3:8]:
        copy.wait()
    taps[:, 0:qk_width] = qk_taps_ref[0].astype(F32)
    taps[:, qk_width : 2 * qk_width] = qk_taps_ref[1].astype(F32)
    taps[:, 2 * qk_width :] = v_taps_ref[...].astype(F32)
    spans = ((q_ref, rim_q, 0), (k_ref, rim_k, qk_width), (v_ref, rim_v, 2 * qk_width))
    for ref, _, start in spans:
        ext[8 : 8 + length, start : start + ref.shape[1]] = ref[...].astype(F32)

    @pl.when(has_prev)
    def _():
        for copy in rims:
            copy.wait_recv()
        for _, rim, start in spans:
            ext[0:8, start : start + rim.shape[1]] = rim[...].astype(F32)[RIM - 8 : RIM]

    @pl.when(jnp.logical_not(has_prev))
    def _():
        ext[0:8, :] = jnp.zeros((8, ext.shape[1]), F32)

    @pl.when(is_chain & jnp.logical_not(chain_prev))
    def _():
        entry[...] = jnp.zeros_like(entry)

    def per_head(src, dst, send, recv, offset):
        def copy_of(h):
            return pltpu.make_async_remote_copy(
                src_ref=src.at[h],
                dst_ref=dst.at[h],
                send_sem=send.at[h],
                recv_sem=recv.at[h],
                device_id=at(offset),
                device_id_type=MESH,
            )

        return copy_of

    near_copy = per_head(map_ref, near_map, near_send, near_recv, 1)
    joined_copy = per_head(joined_out, joined_in, joined_send, joined_recv, 2)
    entry_copy = per_head(entry_out, entry, entry_send, entry_recv, PLANE)
    fan_copy = per_head(entry, entry, fan_send, fan_recv, -2)
    mate_copy = per_head(mate_out, state_in, mate_send, mate_recv, -1)
    relay_copy = per_head(entry, state_in, mate_send, mate_recv, -1)

    def conv(start):
        lanes = pl.ds(pl.multiple_of(start, HDIM), HDIM)
        result = taps[0:1, lanes] * ext[5 : 5 + length, lanes]
        for offset in range(1, CONV):
            result += taps[offset : offset + 1, lanes] * ext[5 + offset : 5 + offset + length, lanes]
        return silu(result)

    def unit(values):
        return values * lax.rsqrt(jnp.sum(values * values, axis=-1, keepdims=True) + 1e-06)

    key_heads = heads // ratio
    key_group = largest(key_heads, 4)

    def local_step(group, _):
        owns = [group * key_group + i for i in range(key_group)]
        queries = [unit(conv(own * HDIM)) * HDIM ** (-0.5) for own in owns]
        keys = [unit(conv(qk_width + own * HDIM)) for own in owns]
        keys_t = [key.T for key in keys]
        key_keys = [mm(key, key_t) for key, key_t in zip(keys, keys_t)]
        query_keys = [mm(query, key_t) for query, key_t in zip(queries, keys_t)]
        upto = row >= col
        lowers, scores, rights, lifts, tails, lasts = [], [], [], [], [], []
        for i in range(key_group * ratio):
            h, k = group * (key_group * ratio) + i, i // ratio
            gamma_r = gamma_rows[pl.ds(h, 1), :]
            beta_r = beta_rows[pl.ds(h, 1), :]
            gamma_c = jnp.broadcast_to(gamma_r, (HDIM, HDIM)).T
            faded = jnp.exp(jnp.where(upto, gamma_c - gamma_r, 0.0)) * beta_r
            lowers.append(jnp.where(row > col, faded * key_keys[k], 0.0).astype(BF16))
            scores.append(jnp.where(upto, faded * query_keys[k], 0.0).astype(BF16))
            growth = jnp.exp(gamma_c)
            last = gamma_c[HDIM - 1 : HDIM, :]
            value = conv(2 * qk_width + h * HDIM)
            rights.append(jnp.concatenate([value, growth * keys[k]], axis=1).astype(BF16))
            lifts.append(growth * queries[k])
            tails.append((keys_t[k] * (jnp.exp(last - gamma_r) * beta_r)).astype(BF16))
            lasts.append(jnp.exp(last))
        eye = jnp.where(row == col, 1.0, 0.0).astype(BF16)
        masks = [masks_ref[level] for level in range(masks_ref.shape[0])]
        inverses = unit_inverses(lowers, masks, eye)
        solved = [mm(inv, right).astype(BF16) for inv, right in zip(inverses, rights)]
        pushes = [mm(tail, one) for tail, one in zip(tails, solved)]
        raises = [mm(score, one) for score, one in zip(scores, solved)]
        for i in range(key_group * ratio):
            h = group * (key_group * ratio) + i
            kept = jnp.where(row == col, lasts[i], 0.0) - pushes[i][:, HDIM:]
            map_ref[h] = jnp.concatenate([kept, pushes[i][:, :HDIM]], axis=1).astype(BF16)
            lift_ref[h] = (lifts[i] - raises[i][:, HDIM:]).astype(BF16)
            local_ref[h] = raises[i][:, :HDIM]
        first = group * (key_group * ratio)

        @pl.when(is_even)
        def _():
            for i in range(key_group * ratio):
                near_copy(first + i).start()

        @pl.when(is_joiner)
        def _():
            for i in range(key_group * ratio):
                near_copy(first + i).wait_recv()
            for i in range(key_group * ratio):
                own = map_ref[first + i]
                moved = mm(own[:, :HDIM], near_map[first + i])
                push = moved[:, HDIM:] + own[:, HDIM:].astype(F32)
                joined_out[first + i] = jnp.concatenate([moved[:, :HDIM], push], axis=1).astype(BF16)
                joined_copy(first + i).start()

        return 0

    lax.fori_loop(0, key_heads // key_group, local_step, 0)

    def apply(pair, state):
        return (mm(pair[:, :HDIM], state) + pair[:, HDIM:].astype(F32)).astype(BF16)

    for copy in ins[8:11]:
        copy.wait()

    def open_gate(h, _):
        lanes = pl.ds(pl.multiple_of(h * HDIM, HDIM), HDIM)
        gates[:, lanes] = gain_ref[...] * silu(gate_ref[:, lanes].astype(F32))
        return 0

    lax.fori_loop(0, heads, open_gate, 0)
    total[...] = jnp.zeros_like(total)

    @pl.when(is_chain)
    def _():
        def step(pair, _):
            both = (2 * pair, 2 * pair + 1)
            for h in both:
                near_copy(h).wait_recv()
                joined_copy(h).wait_recv()

            @pl.when(chain_prev)
            def _():
                for h in both:
                    entry_copy(h).wait_recv()

            for h in both:
                fan_copy(h).start()
            seconds = [apply(joined_in[h], entry[h]) for h in both]
            for h, second in zip(both, seconds):
                mate_out[h] = second
            thirds = [apply(near_map[h], second) for h, second in zip(both, seconds)]
            for h, third in zip(both, thirds):
                state_in[h] = third

            @pl.when(chain_next)
            def _():
                for h in both:
                    entry_out[h] = apply(map_ref[h], state_in[h])
                for h in both:
                    entry_copy(h).start()

            for h in both:
                mate_copy(h).start()
            return 0

        lax.fori_loop(0, heads // 2, step, 0)

    sweep_group = largest(heads, 4)
    sweeps = heads // sweep_group
    depth = sweep_group * HDIM

    def normed_group(group):
        first = group * sweep_group

        @pl.when(is_even)
        def _():
            for i in range(sweep_group):
                mate_copy(first + i).wait_recv()

        @pl.when(is_joiner)
        def _():
            for i in range(sweep_group):
                fan_copy(first + i).wait_recv()
                relay_copy(first + i).start()
            for i in range(sweep_group):
                state_in[first + i] = apply(near_map[first + i], entry[first + i])

        cores = [
            local_ref[first + i]
            + jnp.dot(lift_ref[first + i], state_in[first + i], preferred_element_type=F32)
            for i in range(sweep_group)
        ]
        scales = [lax.rsqrt(jnp.mean(core * core, axis=-1, keepdims=True) + 1e-06) for core in cores]
        normed = [
            core * scale * gates[:, pl.ds(pl.multiple_of((first + i) * HDIM, HDIM), HDIM)]
            for i, (core, scale) in enumerate(zip(cores, scales))
        ]
        return jnp.concatenate(normed, axis=1).astype(BF16)

    def product(normed, group, chunk):
        rows = pl.ds(pl.multiple_of(group * depth, depth), depth)
        weight = w_ref[rows, chunk * chunk_width : (chunk + 1) * chunk_width]
        return jnp.dot(normed, weight, preferred_element_type=F32)

    def sweep(group, _):
        normed = normed_group(group)
        for chunk in range(chunks):
            total[chunk] += product(normed, group, chunk)
        return 0

    lax.fori_loop(0, sweeps - 1, sweep, 0)

    normed = normed_group(sweeps - 1)
    copies = []
    for chunk in range(chunks):
        part[chunk] = (total[chunk] + product(normed, sweeps - 1, chunk)).astype(BF16)
        for hop in range(1, n_head):
            peer = lax.rem(head + hop, n_head)
            copy = pltpu.make_async_remote_copy(
                src_ref=part.at[chunk, pl.ds(pl.multiple_of(peer * rows_out, 16), rows_out), :],
                dst_ref=part_in.at[hop - 1, chunk],
                send_sem=part_send.at[hop - 1, chunk],
                recv_sem=part_recv.at[hop - 1, chunk],
                device_id=(ctx, peer),
                device_id_type=MESH,
            )
            copy.start()
            copies.append((chunk, hop - 1, copy))
    kept = pl.ds(pl.multiple_of(head * rows_out, 16), rows_out)
    for chunk in range(chunks):
        mixed = part[chunk, kept, :].astype(F32)
        for own, hop, copy in copies:
            if own == chunk:
                copy.wait_recv()
                mixed += part_in[hop, chunk].astype(F32)
        out_ref[:, chunk * chunk_width : (chunk + 1) * chunk_width] = mixed.astype(BF16)

    for _, _, copy in copies:
        copy.wait_send()

    @pl.when(has_next)
    def _():
        for copy in rims:
            copy.wait_send()

    sent = (
        (near_copy, is_even),
        (joined_copy, is_joiner),
        (relay_copy, is_joiner),
        (entry_copy, chain_next),
        (fan_copy, is_chain),
        (mate_copy, is_chain),
    )
    for copy_of, mine in sent:

        @pl.when(mine)
        def _(copy_of=copy_of):
            def drain(h, _):
                copy_of(h).wait_send()
                return 0

            lax.fori_loop(0, heads, drain, 0)


def local(n_ctx, n_head, *args):
    (q, k, v, qk_taps, v_taps, gate, beta, rate, log_rate, gain, weight) = args
    length, qk_width = q.shape
    v_width = v.shape[1]
    heads = v_width // HDIM
    model = weight.shape[1]
    rows_out = length // n_head
    width = 2 * qk_width + v_width
    dma = pltpu.SemaphoreType.DMA
    blocks = (heads, HDIM, HDIM)
    peers = max(n_head - 1, 1)
    chunks = 4
    operands = (
        q, k, v, qk_taps, v_taps, gate, beta.T, rate.T, log_rate[None, :], gain[None, :], weight
    )
    return pl.pallas_call(
        functools.partial(layer_kernel, n_ctx, n_head),
        out_shape=jax.ShapeDtypeStruct((rows_out, model), BF16),
        in_specs=[pl.BlockSpec(memory_space=pl.ANY)] * len(operands),
        out_specs=pl.BlockSpec(memory_space=pltpu.VMEM),
        scratch_shapes=[
            *[pltpu.VMEM(operand.shape, operand.dtype) for operand in operands],
            dma((len(operands),)),
            pltpu.VMEM((8 + length, width), F32),
            pltpu.VMEM((RIM, qk_width), BF16),
            pltpu.VMEM((RIM, qk_width), BF16),
            pltpu.VMEM((RIM, v_width), BF16),
            pltpu.VMEM((CONV, width), F32),
            pltpu.VMEM((HDIM, HDIM), F32),
            pltpu.VMEM((HDIM.bit_length() - 1, HDIM, HDIM), BF16),
            pltpu.VMEM((heads, HDIM), F32),
            pltpu.VMEM((heads, HDIM), F32),
            *[pltpu.VMEM((heads, HDIM, 2 * HDIM), BF16)] * 4,
            pltpu.VMEM(blocks, BF16),
            pltpu.VMEM(blocks, F32),
            *[pltpu.VMEM(blocks, BF16)] * 4,
            pltpu.VMEM((length, v_width), F32),
            pltpu.VMEM((chunks, length, model // chunks), F32),
            pltpu.VMEM((chunks, length, model // chunks), BF16),
            pltpu.VMEM((peers, chunks, rows_out, model // chunks), BF16),
            dma((3,)),
            dma((3,)),
            *[dma((heads,))] * 10,
            dma((peers, chunks)),
            dma((peers, chunks)),
        ],
        compiler_params=pltpu.CompilerParams(
            collective_id=0, has_side_effects=True, vmem_limit_bytes=60 * 2**20
        ),
    )(*operands)


def solution(mesh):
    in_specs = (
        P("ctx", "head"),
        P("ctx", "head"),
        P("ctx", "head"),
        P(None, None, "head"),
        P(None, "head"),
        P("ctx", "head"),
        P("ctx", "head"),
        P("ctx", "head"),
        P("head"),
        P(),
        P("head", None),
    )
    out_specs = P(("ctx", "head"), None)
    return jax.shard_map(
        functools.partial(local, mesh.shape["ctx"], mesh.shape["head"]),
        mesh=mesh,
        in_specs=in_specs,
        out_specs=out_specs,
        check_vma=False,
    )
```

```python
import functools

import jax
import jax.numpy as jnp
from jax import lax
from jax.experimental import pallas as pl
from jax.experimental.pallas import tpu as pltpu
from jax.sharding import PartitionSpec as P

HDIM = 128
CONV = 4
RIM = 16
PLANE = 4
MESH = pl.DeviceIdType.MESH
F32 = jnp.float32
BF16 = jnp.bfloat16


def mm(left, right):
    return jnp.dot(left.astype(BF16), right.astype(BF16), preferred_element_type=F32)


def mm_exact(left, right):
    return jnp.dot(left, right, precision=lax.Precision.HIGHEST, preferred_element_type=F32)


def silu(values):
    return values / (1.0 + jnp.exp(-values))


def unit_inverses(lowers, masks, eye):
    span = lowers[0].shape[0]
    inverses = [eye - lower * masks[0] for lower in lowers]
    level, size = 1, 2
    while size < span:
        mask = masks[level]
        if size < RIM:
            steps = [mm(low * mask, inv).astype(BF16) for low, inv in zip(lowers, inverses)]
            news = [mm(inv, step).astype(BF16) for inv, step in zip(inverses, steps)]
            inverses = [inv - new for inv, new in zip(inverses, news)]
        else:
            cuts = [slice(at, at + size) for at in range(0, span, size)]

            def odd(values):
                return jnp.concatenate([values[cut] for cut in cuts[1::2]], axis=0)

            odd_mask = odd(mask)
            halves = [mm(odd(low) * odd_mask, inv).astype(BF16) for low, inv in zip(lowers, inverses)]
            gap = jnp.zeros((size, span), BF16)
            steps = [
                jnp.concatenate(
                    [part for at in range(0, span // 2, size) for part in (gap, half[at : at + size])],
                    axis=0,
                )
                for half in halves
            ]
            odds = [odd(inv) for inv in inverses]
            news = [own - mm(own, step).astype(BF16) for own, step in zip(odds, steps)]
            inverses = [
                jnp.concatenate(
                    [
                        part
                        for i, cut in enumerate(cuts[0::2])
                        for part in (inv[cut], new[i * size : (i + 1) * size])
                    ],
                    axis=0,
                )
                for inv, new in zip(inverses, news)
            ]
        level, size = level + 1, 2 * size
    return inverses


def largest(count, most):
    while count % most:
        most -= 1
    return most


def layer_kernel(
    n_ctx,
    n_head,
    q_hbm,
    k_hbm,
    v_hbm,
    qk_taps_hbm,
    v_taps_hbm,
    gate_hbm,
    beta_hbm,
    rate_hbm,
    log_rate_hbm,
    gain_hbm,
    w_hbm,
    out_ref,
    q_ref,
    k_ref,
    v_ref,
    qk_taps_ref,
    v_taps_ref,
    gate_ref,
    beta_ref,
    rate_ref,
    log_rate_ref,
    gain_ref,
    w_ref,
    in_sem,
    ext,
    rim_q,
    rim_k,
    rim_v,
    taps,
    square,
    masks_ref,
    gamma_rows,
    beta_rows,
    map_ref,
    near_map,
    joined_out,
    joined_in,
    lift_ref,
    local_ref,
    entry,
    entry_out,
    state_in,
    mate_out,
    gates,
    total,
    part,
    part_in,
    rim_send,
    rim_recv,
    near_send,
    near_recv,
    joined_send,
    joined_recv,
    entry_send,
    entry_recv,
    fan_send,
    fan_recv,
    mate_send,
    mate_recv,
    part_send,
    part_recv,
):
    ctx = lax.axis_index("ctx")
    head = lax.axis_index("head")
    length = q_ref.shape[0]
    qk_width = q_ref.shape[1]
    v_width = v_ref.shape[1]
    heads = v_width // HDIM
    ratio = v_width // qk_width
    rows_out = length // n_head
    chunks, _, chunk_width = part.shape
    has_next = ctx < n_ctx - 1
    has_prev = ctx > 0
    place = lax.rem(ctx, PLANE)
    is_even = lax.rem(place, 2) == 0
    is_odd = jnp.logical_not(is_even)
    is_mid = place == 1
    is_end = place == PLANE - 1
    chain_next = is_odd & (ctx + PLANE < n_ctx)
    chain_prev = is_odd & (ctx >= PLANE)
    other = 4 - 2 * place
    chain_base = jnp.where(is_mid, 2, 0)
    relay_base = 2 - chain_base

    def at(offset):
        return (jnp.clip(ctx + offset, 0, n_ctx - 1), head)

    links = (
        (1, has_next),
        (-1, has_prev),
        (other, is_odd),
        (PLANE, chain_next),
        (-PLANE, chain_prev),
    )

    barrier = pltpu.get_barrier_semaphore()

    neighbours = n_head - 1
    for offset, there in links:
        neighbours += there.astype(jnp.int32)

        @pl.when(there)
        def _(offset=offset):
            pl.semaphore_signal(barrier, inc=1, device_id=at(offset), device_id_type=MESH)

    for hop in range(1, n_head):
        peer = lax.rem(head + hop, n_head)
        pl.semaphore_signal(barrier, inc=1, device_id=(ctx, peer), device_id_type=MESH)

    ins = [
        pltpu.make_async_copy(src, dst, in_sem.at[i])
        for i, (src, dst) in enumerate(
            (
                (rate_hbm, rate_ref),
                (log_rate_hbm, log_rate_ref),
                (beta_hbm, beta_ref),
                (qk_taps_hbm, qk_taps_ref),
                (v_taps_hbm, v_taps_ref),
                (q_hbm, q_ref),
                (k_hbm, k_ref),
                (v_hbm, v_ref),
                (gain_hbm, gain_ref),
                (gate_hbm, gate_ref),
                (w_hbm, w_ref),
            )
        )
    ]
    for copy in ins:
        copy.start()

    pl.semaphore_wait(barrier, neighbours)

    rims = [
        pltpu.make_async_remote_copy(
            src_ref=src.at[pl.ds(length - RIM, RIM), :],
            dst_ref=dst,
            send_sem=rim_send.at[i],
            recv_sem=rim_recv.at[i],
            device_id=at(1),
            device_id_type=MESH,
        )
        for i, (src, dst) in enumerate(((q_hbm, rim_q), (k_hbm, rim_k), (v_hbm, rim_v)))
    ]

    @pl.when(has_next)
    def _():
        for copy in rims:
            copy.start()

    row = lax.broadcasted_iota(jnp.int32, (HDIM, HDIM), 0)
    col = lax.broadcasted_iota(jnp.int32, (HDIM, HDIM), 1)
    size = 1
    for level in range(masks_ref.shape[0]):
        inside = (row // (2 * size) == col // (2 * size)) & (row // size > col // size)
        masks_ref[level] = jnp.where(inside, 1.0, 0.0).astype(BF16)
        size *= 2
    for copy in ins[0:3]:
        copy.wait()
    rate = rate_ref[...]
    soft = jnp.maximum(rate, 0.0) + jnp.log1p(jnp.exp(-jnp.abs(rate)))
    square[...] = jnp.zeros_like(square)
    square[:, 0:heads] = jnp.broadcast_to(log_rate_ref[...], (HDIM, heads))
    decay = -jnp.exp(square[...].T[0:heads]) * soft
    upper = jnp.where(row <= col, 1.0, 0.0)
    gamma_rows[...] = mm_exact(decay, upper)
    beta_rows[...] = 1.0 / (1.0 + jnp.exp(-beta_ref[...]))
    for copy in ins[3:8]:
        copy.wait()
    taps[:, 0:qk_width] = qk_taps_ref[0].astype(F32)
    taps[:, qk_width : 2 * qk_width] = qk_taps_ref[1].astype(F32)
    taps[:, 2 * qk_width :] = v_taps_ref[...].astype(F32)
    spans = ((q_ref, rim_q, 0), (k_ref, rim_k, qk_width), (v_ref, rim_v, 2 * qk_width))
    for ref, _, start in spans:
        ext[8 : 8 + length, start : start + ref.shape[1]] = ref[...].astype(F32)

    @pl.when(has_prev)
    def _():
        for copy in rims:
            copy.wait_recv()
        for _, rim, start in spans:
            ext[0:8, start : start + rim.shape[1]] = rim[...].astype(F32)[RIM - 8 : RIM]

    @pl.when(jnp.logical_not(has_prev))
    def _():
        ext[0:8, :] = jnp.zeros((8, ext.shape[1]), F32)

    @pl.when(is_odd & jnp.logical_not(chain_prev))
    def _():
        def clear(four, _):
            for j in range(2):
                entry[4 * four + chain_base + j] = jnp.zeros((HDIM, HDIM), BF16)
            return 0

        lax.fori_loop(0, heads // 4, clear, 0)

    def per_head(src, dst, send, recv, offset):
        def copy_of(h):
            return pltpu.make_async_remote_copy(
                src_ref=src.at[h],
                dst_ref=dst.at[h],
                send_sem=send.at[h],
                recv_sem=recv.at[h],
                device_id=at(offset),
                device_id_type=MESH,
            )

        return copy_of

    near_copy = per_head(map_ref, near_map, near_send, near_recv, 1)
    joined_copy = per_head(joined_out, joined_in, joined_send, joined_recv, other)
    entry_copy = per_head(entry_out, entry, entry_send, entry_recv, PLANE)
    fan_copy = per_head(entry, entry, fan_send, fan_recv, other)
    fan_made = per_head(mate_out, entry, fan_send, fan_recv, other)
    mate_copy = per_head(mate_out, state_in, mate_send, mate_recv, -1)
    relay_copy = per_head(entry, state_in, mate_send, mate_recv, -1)

    def conv(start):
        lanes = pl.ds(pl.multiple_of(start, HDIM), HDIM)
        result = taps[0:1, lanes] * ext[5 : 5 + length, lanes]
        for offset in range(1, CONV):
            result += taps[offset : offset + 1, lanes] * ext[5 + offset : 5 + offset + length, lanes]
        return silu(result)

    def unit(values):
        return values * lax.rsqrt(jnp.sum(values * values, axis=-1, keepdims=True) + 1e-06)

    key_heads = heads // ratio
    key_group = largest(key_heads, 4)

    def local_step(group, _):
        owns = [group * key_group + i for i in range(key_group)]
        queries = [unit(conv(own * HDIM)) * HDIM ** (-0.5) for own in owns]
        keys = [unit(conv(qk_width + own * HDIM)) for own in owns]
        keys_t = [key.T for key in keys]
        key_keys = [mm(key, key_t) for key, key_t in zip(keys, keys_t)]
        query_keys = [mm(query, key_t) for query, key_t in zip(queries, keys_t)]
        upto = row >= col
        lowers, scores, rights, lifts, tails, lasts = [], [], [], [], [], []
        for i in range(key_group * ratio):
            h, k = group * (key_group * ratio) + i, i // ratio
            gamma_r = gamma_rows[pl.ds(h, 1), :]
            beta_r = beta_rows[pl.ds(h, 1), :]
            gamma_c = jnp.broadcast_to(gamma_r, (HDIM, HDIM)).T
            faded = jnp.exp(jnp.where(upto, gamma_c - gamma_r, 0.0)) * beta_r
            lowers.append(jnp.where(row > col, faded * key_keys[k], 0.0).astype(BF16))
            scores.append(jnp.where(upto, faded * query_keys[k], 0.0).astype(BF16))
            growth = jnp.exp(gamma_c)
            last = gamma_c[HDIM - 1 : HDIM, :]
            value = conv(2 * qk_width + h * HDIM)
            rights.append(jnp.concatenate([value, growth * keys[k]], axis=1).astype(BF16))
            lifts.append(growth * queries[k])
            tails.append((keys_t[k] * (jnp.exp(last - gamma_r) * beta_r)).astype(BF16))
            lasts.append(jnp.exp(last))
        eye = jnp.where(row == col, 1.0, 0.0).astype(BF16)
        masks = [masks_ref[level] for level in range(masks_ref.shape[0])]
        inverses = unit_inverses(lowers, masks, eye)
        solved = [mm(inv, right).astype(BF16) for inv, right in zip(inverses, rights)]
        pushes = [mm(tail, one) for tail, one in zip(tails, solved)]
        raises = [mm(score, one) for score, one in zip(scores, solved)]
        for i in range(key_group * ratio):
            h = group * (key_group * ratio) + i
            kept = jnp.where(row == col, lasts[i], 0.0) - pushes[i][:, HDIM:]
            map_ref[h] = jnp.concatenate([kept, pushes[i][:, :HDIM]], axis=1).astype(BF16)
            lift_ref[h] = (lifts[i] - raises[i][:, HDIM:]).astype(BF16)
            local_ref[h] = raises[i][:, :HDIM]
        first = group * (key_group * ratio)

        @pl.when(is_even)
        def _():
            for i in range(key_group * ratio):
                near_copy(first + i).start()

        @pl.when(is_odd)
        def _():
            for i in range(key_group * ratio):
                near_copy(first + i).wait_recv()
            for i in range(0, key_group * ratio, 4):
                for h in (first + i + relay_base, first + i + relay_base + 1):
                    own = map_ref[h]
                    moved = mm(own[:, :HDIM], near_map[h])
                    push = moved[:, HDIM:] + own[:, HDIM:].astype(F32)
                    joined_out[h] = jnp.concatenate([moved[:, :HDIM], push], axis=1).astype(BF16)
                    joined_copy(h).start()

        return 0

    lax.fori_loop(0, key_heads // key_group, local_step, 0)

    def apply(pair, state):
        return (mm(pair[:, :HDIM], state) + pair[:, HDIM:].astype(F32)).astype(BF16)

    for copy in ins[8:11]:
        copy.wait()

    def open_gate(h, _):
        lanes = pl.ds(pl.multiple_of(h * HDIM, HDIM), HDIM)
        gates[:, lanes] = gain_ref[...] * silu(gate_ref[:, lanes].astype(F32))
        return 0

    lax.fori_loop(0, heads, open_gate, 0)
    total[...] = jnp.zeros_like(total)

    @pl.when(is_odd)
    def _():
        def step(four, _):
            both = (4 * four + chain_base, 4 * four + chain_base + 1)
            for h in both:
                joined_copy(h).wait_recv()

            @pl.when(chain_prev)
            def _():
                for h in both:
                    entry_copy(h).wait_recv()

            @pl.when(is_end)
            def _():
                for h in both:
                    fan_copy(h).start()
                seconds = [apply(joined_in[h], entry[h]) for h in both]
                for h, second in zip(both, seconds):
                    mate_out[h] = second
                thirds = [apply(near_map[h], second) for h, second in zip(both, seconds)]
                for h, third in zip(both, thirds):
                    state_in[h] = third

                @pl.when(chain_next)
                def _():
                    for h in both:
                        entry_out[h] = apply(map_ref[h], state_in[h])
                    for h in both:
                        entry_copy(h).start()

                for h in both:
                    mate_copy(h).start()

            @pl.when(is_mid)
            def _():
                firsts = [apply(near_map[h], entry[h]) for h in both]
                for h, first in zip(both, firsts):
                    state_in[h] = first
                seconds = [apply(map_ref[h], first) for h, first in zip(both, firsts)]
                for h, second in zip(both, seconds):
                    mate_out[h] = second
                for h in both:
                    fan_made(h).start()

                @pl.when(chain_next)
                def _():
                    for h in both:
                        entry_out[h] = apply(joined_in[h], mate_out[h])
                    for h in both:
                        entry_copy(h).start()

                for h in both:
                    relay_copy(h).start()

            return 0

        lax.fori_loop(0, heads // 4, step, 0)

    sweep_group = largest(heads, 4)
    sweeps = heads // sweep_group
    depth = sweep_group * HDIM

    def normed_group(group):
        first = group * sweep_group

        @pl.when(is_even)
        def _():
            for i in range(sweep_group):
                mate_copy(first + i).wait_recv()

        @pl.when(is_odd)
        def _():
            both = (first + relay_base, first + relay_base + 1)
            for h in both:
                fan_copy(h).wait_recv()
                relay_copy(h).start()
            for h in both:
                state_in[h] = apply(near_map[h], entry[h])

        cores = [
            local_ref[first + i]
            + jnp.dot(lift_ref[first + i], state_in[first + i], preferred_element_type=F32)
            for i in range(sweep_group)
        ]
        scales = [lax.rsqrt(jnp.mean(core * core, axis=-1, keepdims=True) + 1e-06) for core in cores]
        normed = [
            core * scale * gates[:, pl.ds(pl.multiple_of((first + i) * HDIM, HDIM), HDIM)]
            for i, (core, scale) in enumerate(zip(cores, scales))
        ]
        return jnp.concatenate(normed, axis=1).astype(BF16)

    def product(normed, group, chunk):
        rows = pl.ds(pl.multiple_of(group * depth, depth), depth)
        weight = w_ref[rows, chunk * chunk_width : (chunk + 1) * chunk_width]
        return jnp.dot(normed, weight, preferred_element_type=F32)

    def sweep(group, _):
        normed = normed_group(group)
        for chunk in range(chunks):
            total[chunk] += product(normed, group, chunk)
        return 0

    lax.fori_loop(0, sweeps - 1, sweep, 0)

    normed = normed_group(sweeps - 1)
    copies = []
    for chunk in range(chunks):
        part[chunk] = (total[chunk] + product(normed, sweeps - 1, chunk)).astype(BF16)
        for hop in range(1, n_head):
            peer = lax.rem(head + hop, n_head)
            copy = pltpu.make_async_remote_copy(
                src_ref=part.at[chunk, pl.ds(pl.multiple_of(peer * rows_out, 16), rows_out), :],
                dst_ref=part_in.at[hop - 1, chunk],
                send_sem=part_send.at[hop - 1, chunk],
                recv_sem=part_recv.at[hop - 1, chunk],
                device_id=(ctx, peer),
                device_id_type=MESH,
            )
            copy.start()
            copies.append((chunk, hop - 1, copy))
    kept = pl.ds(pl.multiple_of(head * rows_out, 16), rows_out)
    for chunk in range(chunks):
        mixed = part[chunk, kept, :].astype(F32)
        for own, hop, copy in copies:
            if own == chunk:
                copy.wait_recv()
                mixed += part_in[hop, chunk].astype(F32)
        out_ref[:, chunk * chunk_width : (chunk + 1) * chunk_width] = mixed.astype(BF16)

    for _, _, copy in copies:
        copy.wait_send()

    @pl.when(has_next)
    def _():
        for copy in rims:
            copy.wait_send()

    @pl.when(is_even)
    def _():
        def drain(h, _):
            near_copy(h).wait_send()
            return 0

        lax.fori_loop(0, heads, drain, 0)

    @pl.when(is_odd)
    def _():
        def drain(four, _):
            for j in range(2):
                joined_copy(4 * four + relay_base + j).wait_send()
                fan_copy(4 * four + chain_base + j).wait_send()
            for j in range(4):
                relay_copy(4 * four + j).wait_send()
            return 0

        lax.fori_loop(0, heads // 4, drain, 0)

    @pl.when(chain_next)
    def _():
        def drain(four, _):
            for j in range(2):
                entry_copy(4 * four + chain_base + j).wait_send()
            return 0

        lax.fori_loop(0, heads // 4, drain, 0)


def local(n_ctx, n_head, *args):
    (q, k, v, qk_taps, v_taps, gate, beta, rate, log_rate, gain, weight) = args
    length, qk_width = q.shape
    v_width = v.shape[1]
    heads = v_width // HDIM
    model = weight.shape[1]
    rows_out = length // n_head
    width = 2 * qk_width + v_width
    dma = pltpu.SemaphoreType.DMA
    blocks = (heads, HDIM, HDIM)
    peers = max(n_head - 1, 1)
    chunks = 4
    operands = (
        q, k, v, qk_taps, v_taps, gate, beta.T, rate.T, log_rate[None, :], gain[None, :], weight
    )
    return pl.pallas_call(
        functools.partial(layer_kernel, n_ctx, n_head),
        out_shape=jax.ShapeDtypeStruct((rows_out, model), BF16),
        in_specs=[pl.BlockSpec(memory_space=pl.ANY)] * len(operands),
        out_specs=pl.BlockSpec(memory_space=pltpu.VMEM),
        scratch_shapes=[
            *[pltpu.VMEM(operand.shape, operand.dtype) for operand in operands],
            dma((len(operands),)),
            pltpu.VMEM((8 + length, width), F32),
            pltpu.VMEM((RIM, qk_width), BF16),
            pltpu.VMEM((RIM, qk_width), BF16),
            pltpu.VMEM((RIM, v_width), BF16),
            pltpu.VMEM((CONV, width), F32),
            pltpu.VMEM((HDIM, HDIM), F32),
            pltpu.VMEM((HDIM.bit_length() - 1, HDIM, HDIM), BF16),
            pltpu.VMEM((heads, HDIM), F32),
            pltpu.VMEM((heads, HDIM), F32),
            *[pltpu.VMEM((heads, HDIM, 2 * HDIM), BF16)] * 4,
            pltpu.VMEM(blocks, BF16),
            pltpu.VMEM(blocks, F32),
            *[pltpu.VMEM(blocks, BF16)] * 4,
            pltpu.VMEM((length, v_width), F32),
            pltpu.VMEM((chunks, length, model // chunks), F32),
            pltpu.VMEM((chunks, length, model // chunks), BF16),
            pltpu.VMEM((peers, chunks, rows_out, model // chunks), BF16),
            dma((3,)),
            dma((3,)),
            *[dma((heads,))] * 10,
            dma((peers, chunks)),
            dma((peers, chunks)),
        ],
        compiler_params=pltpu.CompilerParams(
            collective_id=0, has_side_effects=True, vmem_limit_bytes=60 * 2**20
        ),
    )(*operands)


def solution(mesh):
    in_specs = (
        P("ctx", "head"),
        P("ctx", "head"),
        P("ctx", "head"),
        P(None, None, "head"),
        P(None, "head"),
        P("ctx", "head"),
        P("ctx", "head"),
        P("ctx", "head"),
        P("head"),
        P(),
        P("head", None),
    )
    out_specs = P(("ctx", "head"), None)
    return jax.shard_map(
        functools.partial(local, mesh.shape["ctx"], mesh.shape["head"]),
        mesh=mesh,
        in_specs=in_specs,
        out_specs=out_specs,
        check_vma=False,
    )
```

```python
import functools

import jax
import jax.numpy as jnp
from jax import lax
from jax.experimental import pallas as pl
from jax.experimental.pallas import tpu as pltpu
from jax.sharding import PartitionSpec as P

HDIM = 128
CONV = 4
RIM = 16
PLANE = 4
MESH = pl.DeviceIdType.MESH
F32 = jnp.float32
BF16 = jnp.bfloat16


def mm(left, right):
    return jnp.dot(left.astype(BF16), right.astype(BF16), preferred_element_type=F32)


def mm_exact(left, right):
    return jnp.dot(left, right, precision=lax.Precision.HIGHEST, preferred_element_type=F32)


def silu(values):
    return values / (1.0 + jnp.exp(-values))


def unit_inverses(lowers, masks, eye):
    span = lowers[0].shape[0]
    inverses = [eye - lower * masks[0] for lower in lowers]
    level, size = 1, 2
    while size < span:
        mask = masks[level]
        if size < RIM:
            steps = [mm(low * mask, inv).astype(BF16) for low, inv in zip(lowers, inverses)]
            news = [mm(inv, step).astype(BF16) for inv, step in zip(inverses, steps)]
            inverses = [inv - new for inv, new in zip(inverses, news)]
        else:
            cuts = [slice(at, at + size) for at in range(0, span, size)]

            def odd(values):
                return jnp.concatenate([values[cut] for cut in cuts[1::2]], axis=0)

            odd_mask = odd(mask)
            halves = [mm(odd(low) * odd_mask, inv).astype(BF16) for low, inv in zip(lowers, inverses)]
            gap = jnp.zeros((size, span), BF16)
            steps = [
                jnp.concatenate(
                    [part for at in range(0, span // 2, size) for part in (gap, half[at : at + size])],
                    axis=0,
                )
                for half in halves
            ]
            odds = [odd(inv) for inv in inverses]
            news = [own - mm(own, step).astype(BF16) for own, step in zip(odds, steps)]
            inverses = [
                jnp.concatenate(
                    [
                        part
                        for i, cut in enumerate(cuts[0::2])
                        for part in (inv[cut], new[i * size : (i + 1) * size])
                    ],
                    axis=0,
                )
                for inv, new in zip(inverses, news)
            ]
        level, size = level + 1, 2 * size
    return inverses


def largest(count, most):
    while count % most:
        most -= 1
    return most


def layer_kernel(
    n_ctx,
    n_head,
    q_hbm,
    k_hbm,
    v_hbm,
    qk_taps_hbm,
    v_taps_hbm,
    gate_hbm,
    beta_hbm,
    rate_hbm,
    log_rate_hbm,
    gain_hbm,
    w_hbm,
    out_ref,
    q_ref,
    k_ref,
    v_ref,
    qk_taps_ref,
    v_taps_ref,
    gate_ref,
    beta_ref,
    rate_ref,
    log_rate_ref,
    gain_ref,
    w_ref,
    in_sem,
    ext,
    rim_q,
    rim_k,
    rim_v,
    taps,
    square,
    masks_ref,
    gamma_rows,
    beta_rows,
    map_ref,
    near_map,
    joined_out,
    joined_in,
    lift_ref,
    local_ref,
    entry,
    entry_out,
    state_in,
    mate_out,
    gates,
    total,
    part,
    part_in,
    rim_send,
    rim_recv,
    near_send,
    near_recv,
    joined_send,
    joined_recv,
    entry_send,
    entry_recv,
    fan_send,
    fan_recv,
    mate_send,
    mate_recv,
    part_send,
    part_recv,
):
    ctx = lax.axis_index("ctx")
    head = lax.axis_index("head")
    length = q_ref.shape[0]
    qk_width = q_ref.shape[1]
    v_width = v_ref.shape[1]
    heads = v_width // HDIM
    ratio = v_width // qk_width
    rows_out = length // n_head
    chunks, _, chunk_width = part.shape
    has_next = ctx < n_ctx - 1
    has_prev = ctx > 0
    place = lax.rem(ctx, PLANE)
    is_even = lax.rem(place, 2) == 0
    is_odd = jnp.logical_not(is_even)
    is_mid = place == 1
    is_end = place == PLANE - 1
    chain_next = is_odd & (ctx + PLANE < n_ctx)
    chain_prev = is_odd & (ctx >= PLANE)
    other = 4 - 2 * place
    chain_base = jnp.where(is_mid, 2, 0)
    relay_base = 2 - chain_base

    def at(offset):
        return (jnp.clip(ctx + offset, 0, n_ctx - 1), head)

    links = (
        (1, has_next),
        (-1, has_prev),
        (other, is_odd),
        (PLANE, chain_next),
        (-PLANE, chain_prev),
    )

    barrier = pltpu.get_barrier_semaphore()

    neighbours = n_head - 1
    for offset, there in links:
        neighbours += there.astype(jnp.int32)

        @pl.when(there)
        def _(offset=offset):
            pl.semaphore_signal(barrier, inc=1, device_id=at(offset), device_id_type=MESH)

    for hop in range(1, n_head):
        peer = lax.rem(head + hop, n_head)
        pl.semaphore_signal(barrier, inc=1, device_id=(ctx, peer), device_id_type=MESH)

    ins = [
        pltpu.make_async_copy(src, dst, in_sem.at[i])
        for i, (src, dst) in enumerate(
            (
                (rate_hbm, rate_ref),
                (log_rate_hbm, log_rate_ref),
                (beta_hbm, beta_ref),
                (qk_taps_hbm, qk_taps_ref),
                (v_taps_hbm, v_taps_ref),
                (q_hbm, q_ref),
                (k_hbm, k_ref),
                (v_hbm, v_ref),
                (gain_hbm, gain_ref),
                (gate_hbm, gate_ref),
                (w_hbm, w_ref),
            )
        )
    ]
    for copy in ins:
        copy.start()

    pl.semaphore_wait(barrier, neighbours)

    rims = [
        pltpu.make_async_remote_copy(
            src_ref=src.at[pl.ds(length - RIM, RIM), :],
            dst_ref=dst,
            send_sem=rim_send.at[i],
            recv_sem=rim_recv.at[i],
            device_id=at(1),
            device_id_type=MESH,
        )
        for i, (src, dst) in enumerate(((q_hbm, rim_q), (k_hbm, rim_k), (v_hbm, rim_v)))
    ]

    @pl.when(has_next)
    def _():
        for copy in rims:
            copy.start()

    row = lax.broadcasted_iota(jnp.int32, (HDIM, HDIM), 0)
    col = lax.broadcasted_iota(jnp.int32, (HDIM, HDIM), 1)
    size = 1
    for level in range(masks_ref.shape[0]):
        inside = (row // (2 * size) == col // (2 * size)) & (row // size > col // size)
        masks_ref[level] = jnp.where(inside, 1.0, 0.0).astype(BF16)
        size *= 2
    for copy in ins[0:3]:
        copy.wait()
    rate = rate_ref[...]
    soft = jnp.maximum(rate, 0.0) + jnp.log1p(jnp.exp(-jnp.abs(rate)))
    square[...] = jnp.zeros_like(square)
    square[:, 0:heads] = jnp.broadcast_to(log_rate_ref[...], (HDIM, heads))
    decay = -jnp.exp(square[...].T[0:heads]) * soft
    upper = jnp.where(row <= col, 1.0, 0.0)
    gamma_rows[...] = mm_exact(decay, upper)
    beta_rows[...] = 1.0 / (1.0 + jnp.exp(-beta_ref[...]))
    for copy in ins[3:8]:
        copy.wait()
    taps[:, 0:qk_width] = qk_taps_ref[0].astype(F32)
    taps[:, qk_width : 2 * qk_width] = qk_taps_ref[1].astype(F32)
    taps[:, 2 * qk_width :] = v_taps_ref[...].astype(F32)
    spans = ((q_ref, rim_q, 0), (k_ref, rim_k, qk_width), (v_ref, rim_v, 2 * qk_width))
    for ref, _, start in spans:
        ext[8 : 8 + length, start : start + ref.shape[1]] = ref[...].astype(F32)

    @pl.when(has_prev)
    def _():
        for copy in rims:
            copy.wait_recv()
        for _, rim, start in spans:
            ext[0:8, start : start + rim.shape[1]] = rim[...].astype(F32)[RIM - 8 : RIM]

    @pl.when(jnp.logical_not(has_prev))
    def _():
        ext[0:8, :] = jnp.zeros((8, ext.shape[1]), F32)

    @pl.when(is_odd & jnp.logical_not(chain_prev))
    def _():
        def clear(four, _):
            for j in range(2):
                entry[4 * four + chain_base + j] = jnp.zeros((HDIM, HDIM), BF16)
            return 0

        lax.fori_loop(0, heads // 4, clear, 0)

    def per_head(src, dst, send, recv, offset):
        def copy_of(h):
            return pltpu.make_async_remote_copy(
                src_ref=src.at[h],
                dst_ref=dst.at[h],
                send_sem=send.at[h],
                recv_sem=recv.at[h],
                device_id=at(offset),
                device_id_type=MESH,
            )

        return copy_of

    near_copy = per_head(map_ref, near_map, near_send, near_recv, 1)
    joined_copy = per_head(joined_out, joined_in, joined_send, joined_recv, other)
    entry_copy = per_head(entry_out, entry, entry_send, entry_recv, PLANE)
    fan_copy = per_head(entry, entry, fan_send, fan_recv, other)
    fan_made = per_head(mate_out, entry, fan_send, fan_recv, other)
    mate_copy = per_head(mate_out, state_in, mate_send, mate_recv, -1)
    relay_copy = per_head(entry, state_in, mate_send, mate_recv, -1)

    def conv(start):
        lanes = pl.ds(pl.multiple_of(start, HDIM), HDIM)
        result = taps[0:1, lanes] * ext[5 : 5 + length, lanes]
        for offset in range(1, CONV):
            result += taps[offset : offset + 1, lanes] * ext[5 + offset : 5 + offset + length, lanes]
        return silu(result)

    def unit(values):
        return values * lax.rsqrt(jnp.sum(values * values, axis=-1, keepdims=True) + 1e-06)

    key_heads = heads // ratio
    key_group = largest(key_heads, 2)
    groups = key_heads // key_group

    def join(group):
        first = group * (key_group * ratio)
        for i in range(key_group * ratio):
            near_copy(first + i).wait_recv()
        for i in range(0, key_group * ratio, 4):
            for h in (first + i + relay_base, first + i + relay_base + 1):
                own = map_ref[h]
                moved = mm(own[:, :HDIM], near_map[h])
                push = moved[:, HDIM:] + own[:, HDIM:].astype(F32)
                joined_out[h] = jnp.concatenate([moved[:, :HDIM], push], axis=1).astype(BF16)
                joined_copy(h).start()

    def local_step(group, _):
        owns = [group * key_group + i for i in range(key_group)]
        queries = [unit(conv(own * HDIM)) * HDIM ** (-0.5) for own in owns]
        keys = [unit(conv(qk_width + own * HDIM)) for own in owns]
        keys_t = [key.T for key in keys]
        key_keys = [mm(key, key_t) for key, key_t in zip(keys, keys_t)]
        query_keys = [mm(query, key_t) for query, key_t in zip(queries, keys_t)]
        upto = row >= col
        lowers, scores, rights, lifts, tails, lasts = [], [], [], [], [], []
        for i in range(key_group * ratio):
            h, k = group * (key_group * ratio) + i, i // ratio
            gamma_r = gamma_rows[pl.ds(h, 1), :]
            beta_r = beta_rows[pl.ds(h, 1), :]
            gamma_c = jnp.broadcast_to(gamma_r, (HDIM, HDIM)).T
            faded = jnp.exp(jnp.where(upto, gamma_c - gamma_r, 0.0)) * beta_r
            lowers.append(jnp.where(row > col, faded * key_keys[k], 0.0).astype(BF16))
            scores.append(jnp.where(upto, faded * query_keys[k], 0.0).astype(BF16))
            growth = jnp.exp(gamma_c)
            last = gamma_c[HDIM - 1 : HDIM, :]
            value = conv(2 * qk_width + h * HDIM)
            rights.append(jnp.concatenate([value, growth * keys[k]], axis=1).astype(BF16))
            lifts.append(growth * queries[k])
            tails.append((keys_t[k] * (jnp.exp(last - gamma_r) * beta_r)).astype(BF16))
            lasts.append(jnp.exp(last))
        eye = jnp.where(row == col, 1.0, 0.0).astype(BF16)
        masks = [masks_ref[level] for level in range(masks_ref.shape[0])]
        inverses = unit_inverses(lowers, masks, eye)
        solved = [mm(inv, right).astype(BF16) for inv, right in zip(inverses, rights)]
        pushes = [mm(tail, one) for tail, one in zip(tails, solved)]
        raises = [mm(score, one) for score, one in zip(scores, solved)]
        for i in range(key_group * ratio):
            h = group * (key_group * ratio) + i
            kept = jnp.where(row == col, lasts[i], 0.0) - pushes[i][:, HDIM:]
            map_ref[h] = jnp.concatenate([kept, pushes[i][:, :HDIM]], axis=1).astype(BF16)
            lift_ref[h] = (lifts[i] - raises[i][:, HDIM:]).astype(BF16)
            local_ref[h] = raises[i][:, :HDIM]
        first = group * (key_group * ratio)

        @pl.when(is_even)
        def _():
            for i in range(key_group * ratio):
                near_copy(first + i).start()

        @pl.when(is_odd & (group > 0))
        def _():
            join(group - 1)

        return 0

    lax.fori_loop(0, groups, local_step, 0)

    @pl.when(is_odd)
    def _():
        join(groups - 1)

    def apply(pair, state):
        return (mm(pair[:, :HDIM], state) + pair[:, HDIM:].astype(F32)).astype(BF16)

    for copy in ins[8:11]:
        copy.wait()

    def open_gate(h, _):
        lanes = pl.ds(pl.multiple_of(h * HDIM, HDIM), HDIM)
        gates[:, lanes] = gain_ref[...] * silu(gate_ref[:, lanes].astype(F32))
        return 0

    lax.fori_loop(0, heads, open_gate, 0)
    total[...] = jnp.zeros_like(total)

    @pl.when(is_odd)
    def _():
        def step(four, _):
            both = (4 * four + chain_base, 4 * four + chain_base + 1)
            for h in both:
                joined_copy(h).wait_recv()

            @pl.when(chain_prev)
            def _():
                for h in both:
                    entry_copy(h).wait_recv()

            @pl.when(is_end)
            def _():
                for h in both:
                    fan_copy(h).start()
                seconds = [apply(joined_in[h], entry[h]) for h in both]
                for h, second in zip(both, seconds):
                    mate_out[h] = second
                thirds = [apply(near_map[h], second) for h, second in zip(both, seconds)]
                for h, third in zip(both, thirds):
                    state_in[h] = third

                @pl.when(chain_next)
                def _():
                    for h in both:
                        entry_out[h] = apply(map_ref[h], state_in[h])
                    for h in both:
                        entry_copy(h).start()

                for h in both:
                    mate_copy(h).start()

            @pl.when(is_mid)
            def _():
                firsts = [apply(near_map[h], entry[h]) for h in both]
                for h, first in zip(both, firsts):
                    state_in[h] = first
                seconds = [apply(map_ref[h], first) for h, first in zip(both, firsts)]
                for h, second in zip(both, seconds):
                    mate_out[h] = second
                for h in both:
                    fan_made(h).start()

                @pl.when(chain_next)
                def _():
                    for h in both:
                        entry_out[h] = apply(joined_in[h], mate_out[h])
                    for h in both:
                        entry_copy(h).start()

                for h in both:
                    relay_copy(h).start()

            return 0

        lax.fori_loop(0, heads // 4, step, 0)

    sweep_group = largest(heads, 4)
    sweeps = heads // sweep_group
    depth = sweep_group * HDIM

    def relay(group):
        for h in (group * sweep_group + relay_base, group * sweep_group + relay_base + 1):
            fan_copy(h).wait_recv()
            relay_copy(h).start()

    @pl.when(is_odd)
    def _():
        relay(0)

    def normed_group(group):
        first = group * sweep_group

        @pl.when(is_even)
        def _():
            for i in range(sweep_group):
                mate_copy(first + i).wait_recv()

        @pl.when(is_odd)
        def _():
            both = (first + relay_base, first + relay_base + 1)

            @pl.when(group < sweeps - 1)
            def _():
                relay(group + 1)

            for h in both:
                state_in[h] = apply(near_map[h], entry[h])

        cores = [
            local_ref[first + i]
            + jnp.dot(lift_ref[first + i], state_in[first + i], preferred_element_type=F32)
            for i in range(sweep_group)
        ]
        scales = [lax.rsqrt(jnp.mean(core * core, axis=-1, keepdims=True) + 1e-06) for core in cores]
        normed = [
            core * scale * gates[:, pl.ds(pl.multiple_of((first + i) * HDIM, HDIM), HDIM)]
            for i, (core, scale) in enumerate(zip(cores, scales))
        ]
        return jnp.concatenate(normed, axis=1).astype(BF16)

    def product(normed, group, chunk):
        rows = pl.ds(pl.multiple_of(group * depth, depth), depth)
        weight = w_ref[rows, chunk * chunk_width : (chunk + 1) * chunk_width]
        return jnp.dot(normed, weight, preferred_element_type=F32)

    def sweep(group, _):
        normed = normed_group(group)
        for chunk in range(chunks):
            total[chunk] += product(normed, group, chunk)
        return 0

    lax.fori_loop(0, sweeps - 1, sweep, 0)

    normed = normed_group(sweeps - 1)
    copies = []
    for chunk in range(chunks):
        part[chunk] = (total[chunk] + product(normed, sweeps - 1, chunk)).astype(BF16)
        for hop in range(1, n_head):
            peer = lax.rem(head + hop, n_head)
            copy = pltpu.make_async_remote_copy(
                src_ref=part.at[chunk, pl.ds(pl.multiple_of(peer * rows_out, 16), rows_out), :],
                dst_ref=part_in.at[hop - 1, chunk],
                send_sem=part_send.at[hop - 1, chunk],
                recv_sem=part_recv.at[hop - 1, chunk],
                device_id=(ctx, peer),
                device_id_type=MESH,
            )
            copy.start()
            copies.append((chunk, hop - 1, copy))
    kept = pl.ds(pl.multiple_of(head * rows_out, 16), rows_out)
    for chunk in range(chunks):
        mixed = part[chunk, kept, :].astype(F32)
        for own, hop, copy in copies:
            if own == chunk:
                copy.wait_recv()
                mixed += part_in[hop, chunk].astype(F32)
        out_ref[:, chunk * chunk_width : (chunk + 1) * chunk_width] = mixed.astype(BF16)

    for _, _, copy in copies:
        copy.wait_send()

    @pl.when(has_next)
    def _():
        for copy in rims:
            copy.wait_send()

    @pl.when(is_even)
    def _():
        def drain(h, _):
            near_copy(h).wait_send()
            return 0

        lax.fori_loop(0, heads, drain, 0)

    @pl.when(is_odd)
    def _():
        def drain(four, _):
            for j in range(2):
                joined_copy(4 * four + relay_base + j).wait_send()
                fan_copy(4 * four + chain_base + j).wait_send()
            for j in range(4):
                relay_copy(4 * four + j).wait_send()
            return 0

        lax.fori_loop(0, heads // 4, drain, 0)

    @pl.when(chain_next)
    def _():
        def drain(four, _):
            for j in range(2):
                entry_copy(4 * four + chain_base + j).wait_send()
            return 0

        lax.fori_loop(0, heads // 4, drain, 0)


def local(n_ctx, n_head, *args):
    (q, k, v, qk_taps, v_taps, gate, beta, rate, log_rate, gain, weight) = args
    length, qk_width = q.shape
    v_width = v.shape[1]
    heads = v_width // HDIM
    model = weight.shape[1]
    rows_out = length // n_head
    width = 2 * qk_width + v_width
    dma = pltpu.SemaphoreType.DMA
    blocks = (heads, HDIM, HDIM)
    peers = max(n_head - 1, 1)
    chunks = 4
    operands = (
        q, k, v, qk_taps, v_taps, gate, beta.T, rate.T, log_rate[None, :], gain[None, :], weight
    )
    return pl.pallas_call(
        functools.partial(layer_kernel, n_ctx, n_head),
        out_shape=jax.ShapeDtypeStruct((rows_out, model), BF16),
        in_specs=[pl.BlockSpec(memory_space=pl.ANY)] * len(operands),
        out_specs=pl.BlockSpec(memory_space=pltpu.VMEM),
        scratch_shapes=[
            *[pltpu.VMEM(operand.shape, operand.dtype) for operand in operands],
            dma((len(operands),)),
            pltpu.VMEM((8 + length, width), F32),
            pltpu.VMEM((RIM, qk_width), BF16),
            pltpu.VMEM((RIM, qk_width), BF16),
            pltpu.VMEM((RIM, v_width), BF16),
            pltpu.VMEM((CONV, width), F32),
            pltpu.VMEM((HDIM, HDIM), F32),
            pltpu.VMEM((HDIM.bit_length() - 1, HDIM, HDIM), BF16),
            pltpu.VMEM((heads, HDIM), F32),
            pltpu.VMEM((heads, HDIM), F32),
            *[pltpu.VMEM((heads, HDIM, 2 * HDIM), BF16)] * 4,
            pltpu.VMEM(blocks, BF16),
            pltpu.VMEM(blocks, F32),
            *[pltpu.VMEM(blocks, BF16)] * 4,
            pltpu.VMEM((length, v_width), F32),
            pltpu.VMEM((chunks, length, model // chunks), F32),
            pltpu.VMEM((chunks, length, model // chunks), BF16),
            pltpu.VMEM((peers, chunks, rows_out, model // chunks), BF16),
            dma((3,)),
            dma((3,)),
            *[dma((heads,))] * 10,
            dma((peers, chunks)),
            dma((peers, chunks)),
        ],
        compiler_params=pltpu.CompilerParams(
            collective_id=0, has_side_effects=True, vmem_limit_bytes=60 * 2**20
        ),
    )(*operands)


def solution(mesh):
    in_specs = (
        P("ctx", "head"),
        P("ctx", "head"),
        P("ctx", "head"),
        P(None, None, "head"),
        P(None, "head"),
        P("ctx", "head"),
        P("ctx", "head"),
        P("ctx", "head"),
        P("head"),
        P(),
        P("head", None),
    )
    out_specs = P(("ctx", "head"), None)
    return jax.shard_map(
        functools.partial(local, mesh.shape["ctx"], mesh.shape["head"]),
        mesh=mesh,
        in_specs=in_specs,
        out_specs=out_specs,
        check_vma=False,
    )
```
